256 devices in a mesh: var: 4 (over y), tok: 64 (over x, z, core).
Axes of the slice: x: 4, y: 4, z: 8, core: 2. Of those that a mesh axis runs over, the one named last changes fastest.
Arguments:
- tokens: bfloat16 [8, 16384, 8192], P('var', 'tok'), may hold values from -16 to 16
- up_panel: bfloat16 [8, 8192, 1024], P('var', 'tok'), may hold values from -6 to 6
Outputs:
- gram_sum: float32 [256, 8192], P('var', 'tok')
- numerator: float32 [256, 1024], P(('var', 'tok'))
The draws below stay inside these ranges and needn't reach their ends.
All inputs are finite; a program needn't handle non-finite values.
Results may differ from the reference program's by a relative error of at most 0.00045.
Values may be sent and summed in bfloat16 or wider, within the bound.
A program may use at most 128 MiB of HBM per device.

```python
import jax
import jax.numpy as jnp
from jax import lax

D = 8192
PANEL = 1024
WINDOW = 256
VARIANTS = 8
TOKENS = 16384


def spiked(array, own_key, source, target, parts, factor):
    def block_of(position):
        return (jnp.arange(array.shape[position]) // (array.shape[position] // parts)).reshape((-1,) + (1,) * (array.ndim - 1 - position))

    near = jax.random.permutation(own_key, parts)[block_of(target)]
    other_side = (block_of(target) + parts // 2) % parts
    return jnp.where((block_of(source) == near) | (block_of(source) == other_side), factor * array, array)


def block_scale(stream_key, extent, split, smallest, top_value):
    def one(axis_at, parts):
        draws = jax.random.uniform(jax.random.fold_in(jax.random.fold_in(stream_key, 6), axis_at), (parts,), jnp.float32, smallest / len(split), top_value / len(split))
        return jnp.repeat(jnp.exp(draws), extent[axis_at] // parts).reshape((-1,) + (1,) * (len(extent) - axis_at - 1))

    factor_of = one(*split[0])
    for cut in split[1:]:
        factor_of = factor_of * one(*cut)
    return factor_of


def bell_draw(stream_key, extent, spread, bound, pieces=(), kind=jnp.bfloat16):
    level = block_scale(stream_key, extent, pieces, -0.22, 0.18) if pieces else 1.0
    array = jax.random.normal(stream_key, extent, jnp.float32) * spread * level
    return jnp.minimum(jnp.maximum(array, -bound), bound).astype(kind)


def gaussian_with(stream_key, shape, width, limit, cuts, heavy, held_as=jnp.bfloat16):
    array = width * jax.random.normal(stream_key, shape, jnp.float32)
    if cuts:
        array = array * block_scale(stream_key, shape, cuts, -0.22, 0.18)
    return jnp.clip(spiked(array, jax.random.fold_in(stream_key, 3), *heavy), -limit, limit).astype(held_as)


def setup_inputs(seed: int = 0) -> dict:
    seeds = jax.random.split(jax.random.key(seed), 3)
    return {
        "tokens": gaussian_with(seeds[0], (VARIANTS, TOKENS, D), 1.0, 16.0, ((0, 4), (1, 64)), (1, 2, 64, 4.0)),
        "up_panel": bell_draw(seeds[1], (VARIANTS, D, PANEL), 1.0, 6.0, ((0, 4), (1, 64))),
    }


def reference(tokens, up_panel):
    scale = 1.0 / TOKENS
    gram_total = jnp.zeros((WINDOW, D), jnp.float32)
    numer_total = jnp.zeros((WINDOW, PANEL), jnp.float32)
    for variant in range(VARIANTS):
        rows = tokens[variant]
        gram_one = jnp.dot(rows[:, :WINDOW].T, rows, preferred_element_type=jnp.float32) * scale
        gram_total = gram_total + gram_one
        numer_total = numer_total + jnp.dot(gram_one, up_panel[variant].astype(jnp.float32), precision=lax.Precision.HIGHEST)
    return gram_total, numer_total
```

```python
import functools

import jax
import jax.numpy as jnp
from jax import lax
from jax.experimental import pallas as pl
from jax.experimental.pallas import tpu as pltpu
from jax.sharding import PartitionSpec as P

WINDOW = 256
NX, NZ, NY = 4, 8, 4
CHIPS = NX * NZ
UNIT = 16
UNITS = WINDOW // UNIT
KA = 7
KB = UNITS - KA
K = max(KA, KB)
PIECES = 8
POWER = 9
TOP = 2.0**13.8
MESH = pl.DeviceIdType.MESH
F32, BF16 = jnp.float32, jnp.bfloat16


def encode(value, factor):
    t = value * factor
    t2 = t * t
    t4 = t2 * t2
    return (t4 * t4 * t).astype(BF16)


def decode(code, factor):
    y = code.astype(F32)
    root = jnp.exp2(jnp.log(jnp.maximum(jnp.abs(y), 1e-38)) * (1.4426950408889634 / POWER))
    return jnp.where(y < 0, -root, root) * factor


class Ring:
    def __init__(self, n, blocks, units, me, device, base, source, refs):
        self.n, self.half, self.blocks, self.units = n, n // 2, blocks, units
        self.me, self.device, self.base, self.source = me, device, base, source
        (self.s0, self.sn, self.r0, self.rn, self.bs, self.br, self.enc, self.dec,
         self.send_sem, self.recv_sem, self.bsend_sem, self.brecv_sem) = refs

    @staticmethod
    def scratch(n, blocks, units):
        half = n // 2
        first = pltpu.VMEM((units, 2, blocks, UNIT, 128), BF16)
        later = pltpu.VMEM((units, 2, half - 1, 2, blocks, UNIT, 128), BF16)
        bound = pltpu.VMEM((2, half, UNIT, 128), F32)
        return [first, later, first, later, bound, bound, bound, bound,
                pltpu.SemaphoreType.DMA((2,)), pltpu.SemaphoreType.DMA((units, 2, half)),
                pltpu.SemaphoreType.DMA, pltpu.SemaphoreType.DMA((2, half))]

    def data_copy(self, k, d, s, to):
        if s == 0:
            src, dst = self.s0.at[k, d], self.r0.at[k, d]
        else:
            src, dst = self.sn.at[k, d, s - 1], self.rn.at[k, d, s - 1]
        return pltpu.make_async_remote_copy(
            src_ref=src, dst_ref=dst, send_sem=self.send_sem.at[min(s, 1)],
            recv_sem=self.recv_sem.at[k, d, s], device_id=to, device_id_type=MESH)

    def bound_copy(self, d, s, to):
        return pltpu.make_async_remote_copy(
            src_ref=self.bs.at[d, s], dst_ref=self.br.at[d, s], send_sem=self.bsend_sem,
            recv_sem=self.brecv_sem.at[d, s], device_id=to, device_id_type=MESH)

    def neighbour(self, d):
        return self.device(lax.rem(self.me + (1 if d == 0 else self.n - 1), self.n))

    def arrived(self, k, d, s):
        self.data_copy(k, d, s, self.neighbour(d)).wait_recv()

    def send(self, s, k):
        for d in (0, 1):
            to = self.neighbour(d)
            far = self.half - s
            dest = lax.rem(self.me + (far if d == 0 else self.n - far), self.n)
            if s > 0:
                self.arrived(k, d, s - 1)

            @pl.when(k == 0)
            def _():
                bound = self.base[...]
                if s > 0:
                    self.bound_copy(d, s - 1, to).wait_recv()
                    came = self.br[d, s - 1]
                    self.dec[d, s - 1] = came * (1.0 / TOP)
                    bound = bound + came
                self.bs[d, s] = bound
                self.enc[d, s] = TOP / bound
                self.bound_copy(d, s, to).start()

            enc = self.enc[d, s]
            if s == 0:
                self.s0[k, d] = encode(self.source(dest, d, k), enc)
            else:
                dec = self.dec[d, s - 1]
                for h in (0, 1):
                    value = self.source(dest, h, k)
                    if s > 1:
                        value = value + decode(self.rn[k, d, s - 2, h], dec)
                    elif h == d:
                        value = value + decode(self.r0[k, d], dec)
                    self.sn[k, d, s - 1, h] = encode(value, enc)
            self.data_copy(k, d, s, to).start()

    def finish(self, k, total, store):
        last = self.half - 1
        for d in (0, 1):
            self.arrived(k, d, last)

        @pl.when(k == 0)
        def _():
            for d in (0, 1):
                self.bound_copy(d, last, self.neighbour(d)).wait_recv()
                self.dec[d, last] = self.br[d, last] * (1.0 / TOP)
            if total is not None:
                total[...] = self.base[...] + self.br[0, last] + self.br[1, last]

        for h in (0, 1):
            value = self.source(self.me, h, k)
            for d in (0, 1):
                value = value + decode(self.rn[k, d, last - 1, h], self.dec[d, last])
            store(h, value)

    def sent(self):
        to = self.neighbour(0)
        for src, dst, sem in ((self.s0, self.r0, self.send_sem.at[0]), (self.sn, self.rn, self.send_sem.at[1]),
                              (self.bs, self.br, self.bsend_sem)):
            pltpu.make_async_remote_copy(src_ref=src, dst_ref=dst, send_sem=sem, recv_sem=sem,
                                         device_id=to, device_id_type=MESH).wait_send()


SHAPES = ((NZ, NX, KA), (NX, 1, KA), (NX, NZ, KB), (NZ, 1, KB))


def kernel(scale, tokens, up, gram, num, own, other, wt, upv, prod, base, base_a, base_b, mid_a, mid_b, fin,
           msg1, recv1, msg2, recv2, gacc, own_sem, other_send, other_recv, up_sem, up_send, up_recv,
           send1, sem1, send2, sem2, *ring_refs):
    y, t = lax.axis_index("var"), lax.axis_index("tok")
    c = lax.rem(t, 2)
    chip = t // 2
    z, x = lax.rem(chip, NZ), chip // NZ
    oc = 1 - c
    sibling = (y, chip * 2 + oc)
    width = own.shape[1]
    part = width // PIECES
    depth = own.shape[0]

    def own_copy(i):
        cols = pl.ds(pl.multiple_of(i * part, part), part)
        return pltpu.make_async_copy(tokens.at[c, :, cols], own.at[:, cols], own_sem.at[i])

    def other_copy(i):
        cols = pl.ds(pl.multiple_of(i * part, part), part)
        return pltpu.make_async_remote_copy(
            src_ref=tokens.at[oc, :, cols], dst_ref=other.at[:, cols], send_sem=other_send,
            recv_sem=other_recv.at[i], device_id=sibling, device_id_type=MESH)

    up_own = pltpu.make_async_copy(up.at[c], upv.at[c], up_sem)
    up_other = pltpu.make_async_remote_copy(src_ref=up.at[oc], dst_ref=upv.at[c], send_sem=up_send,
                                            recv_sem=up_recv, device_id=sibling, device_id_type=MESH)
    for i in range(PIECES):
        own_copy(i).start()
    up_own.start()

    barrier = pltpu.get_barrier_semaphore()

    def greet_chip(o, carry):
        pl.semaphore_signal(barrier, inc=1, device_id=(y, lax.rem(chip + o, CHIPS) * 2 + c), device_id_type=MESH)
        return carry

    def pair_of(o):
        pc = lax.rem(y * 2 + c + o, 2 * NY)
        return pc, (pc // 2, chip * 2 + lax.rem(pc, 2))

    def greet_pair(o, carry):
        pl.semaphore_signal(barrier, inc=1, device_id=pair_of(o)[1], device_id_type=MESH)
        return carry

    lax.fori_loop(1, CHIPS, greet_chip, 0)
    lax.fori_loop(1, 2 * NY, greet_pair, 0)
    pl.semaphore_wait(barrier, CHIPS - 1 + 2 * NY - 1)

    for i in range(PIECES):
        other_copy(i).start()
    up_other.start()

    row = lax.broadcasted_iota(jnp.int32, (WINDOW, WINDOW), 0)
    col = lax.broadcasted_iota(jnp.int32, (WINDOW, WINDOW), 1)
    feature = ((row >> 2) & 3) * (WINDOW // NY) + (row >> 4) * 4 + (row & 3)
    pick = jnp.where(col == feature, 1.0, 0.0).astype(BF16)

    def window(ref):
        return lax.dot_general(pick, ref[:, :WINDOW], (((1,), (1,)), ((), ())), preferred_element_type=F32).astype(BF16)

    base[...] = jnp.full(base.shape, 1e-33, F32)
    blocks = part // 256

    def multiply(i, carry):
        own_copy(i).wait()
        other_copy(i).wait_recv()

        @pl.when(i == 0)
        def _():
            wt[:, :depth] = window(own)
            wt[:, depth:] = window(other)

        for j in range(blocks):
            b = i * blocks + j
            cols = pl.ds(pl.multiple_of(b * 256, 256), 256)
            product = jnp.dot(wt[:, :depth], own[:, cols], preferred_element_type=F32)
            product = product + jnp.dot(wt[:, depth:], other[:, cols], preferred_element_type=F32)
            bx, bz = b // NZ, lax.rem(b, NZ)
            prod[bx, bz, 0] = product[:, :128]
            prod[bx, bz, 1] = product[:, 128:]
            top = jnp.max(jnp.abs(product).reshape(UNITS, UNIT, 256), axis=0)
            base[...] = jnp.maximum(base[...], jnp.maximum(top[:, :128], top[:, 128:]))
        return carry

    lax.fori_loop(0, PIECES, multiply, 0)
    up_own.wait()
    up_other.wait_recv()

    count = len(ring_refs) // 4
    refs = [ring_refs[i * count:(i + 1) * count] for i in range(4)]
    along_z = lambda at: (y, (x * NZ + at) * 2 + c)
    along_x = lambda at: (y, (at * NZ + z) * 2 + c)
    rows = lambda u: pl.ds(pl.multiple_of(u * UNIT, UNIT), UNIT)
    az = Ring(*SHAPES[0], z, along_z, base, lambda dest, h, k: prod[:, dest, h, rows(k), :], refs[0])
    ax = Ring(*SHAPES[1], x, along_x, base_a, lambda dest, h, k: mid_a[k, h, pl.ds(dest, 1)], refs[1])
    bx = Ring(*SHAPES[2], x, along_x, base, lambda dest, h, k: prod[dest, :, h, rows(KA + k), :], refs[2])
    bz = Ring(*SHAPES[3], z, along_z, base_b, lambda dest, h, k: mid_b[k, h, pl.ds(dest, 1)], refs[3])

    def numerators(k):
        g = [jnp.concatenate([fin[k, 0, h], fin[k, 1, h]], axis=0) for h in (0, 1)]
        total = None
        for h in (0, 1):
            high = g[h].astype(BF16)
            low = (g[h] - high.astype(F32)).astype(BF16)
            term = jnp.dot(jnp.concatenate([high, low], axis=0), upv[h], preferred_element_type=F32)
            total = term if total is None else total + term
        total = total[:2 * UNIT] + total[2 * UNIT:]
        tiles = total.reshape(2 * UNIT, 8, 128)
        for p in range(NY):
            for half in (0, 1):
                for ab in (0, 1):
                    for i in (0, 1):
                        msg1[k, 2 * p + half, 2 * ab + i] = tiles[UNIT * ab + 4 * p + 2 * i + half]
                    msg1[k, 2 * p + half, 4, 4 * ab:4 * ab + 4, :] = fin[k, ab, half, 4 * p:4 * p + 4, :]

        def post(o, carry):
            pc, to = pair_of(o)
            pltpu.make_async_remote_copy(src_ref=msg1.at[k, pc], dst_ref=recv1.at[k, o - 1], send_sem=send1.at[k],
                                         recv_sem=sem1.at[k], device_id=to, device_id_type=MESH).start()
            return carry

        lax.fori_loop(1, 2 * NY, post, 0)

    def pair_copies(k):
        return pltpu.make_async_remote_copy(src_ref=recv1.at[k], dst_ref=recv1.at[k], send_sem=send1.at[k],
                                            recv_sem=sem1.at[k], device_id=sibling, device_id_type=MESH)

    def row_copy(src, to_chip):
        slot = lax.rem(to_chip - chip + CHIPS, CHIPS) - 1
        return pltpu.make_async_remote_copy(src_ref=src, dst_ref=recv2.at[slot], send_sem=send2, recv_sem=sem2,
                                            device_id=(y, to_chip * 2 + c), device_id_type=MESH)

    def pass_on(k):
        pair_copies(k).wait_recv()
        total = msg1[k, y * 2 + c]
        for o in range(2 * NY - 1):
            total = total + recv1[k, o]
        msg2[k] = total[:4]
        gacc[k] = total[4]
        for ab in (0, 1):

            @pl.when(k < (KA, KB)[ab])
            def _():
                for i in (0, 1):
                    u = k + ab * KA
                    to = (u // 4) * NZ + 2 * lax.rem(u, 4) + i

                    @pl.when(to == chip)
                    def _():
                        recv2[CHIPS - 1] = msg2[k, 2 * ab + i]

                    @pl.when(to != chip)
                    def _():
                        row_copy(msg2.at[k, 2 * ab + i], to).start()

    def put(ref, k):
        def store(h, value):
            ref[k, h] = value
        return store

    def put_final(ab, k):
        def store(h, value):
            fin[k, ab, h] = value[0] * scale
        return store

    for k in range(KA, K):
        fin[k, 0] = jnp.zeros(fin.shape[2:], F32)

    def when(k, units, run):
        pl.when(jnp.logical_and(k >= 0, k < units))(lambda: run(k))

    def az_to_ax(k):
        az.finish(k, base_a, put(mid_a, k))
        ax.send(0, k)

    def bx_to_bz(k):
        bx.finish(k, base_b, put(mid_b, k))
        bz.send(0, k)

    def tick(at, carry):
        a = [functools.partial(az.send, s) for s in range(4)]
        a += [az_to_ax, functools.partial(ax.send, 1), lambda k: ax.finish(k, None, put_final(0, k))]
        b = [functools.partial(bx.send, s) for s in range(2)]
        b += [bx_to_bz] + [functools.partial(bz.send, s) for s in range(1, 4)]
        b += [lambda k: bz.finish(k, None, put_final(1, k))]
        for stage in range(7):
            when(at - stage, KA, a[stage])
            when(at - stage, KB, b[stage])
        when(at - 6, K, numerators)
        when(at - 7, K, pass_on)
        return carry

    lax.fori_loop(0, K + 8, tick, 0)

    for k in range(K):
        if k < KA:
            gram[4 * k:4 * k + 4, :] = gacc[k, 0:4, :]
        if k < KB:
            u = KA + k
            gram[4 * u:4 * u + 4, :] = gacc[k, 4:8, :]
    all_rows = pltpu.make_async_remote_copy(src_ref=recv2.at[pl.ds(0, CHIPS - 1)], dst_ref=recv2.at[pl.ds(0, CHIPS - 1)],
                                            send_sem=send2, recv_sem=sem2, device_id=sibling, device_id_type=MESH)
    all_rows.wait_recv()
    total = jnp.sum(recv2[...], axis=0)
    for i in range(8):
        num[0:1, 128 * i:128 * (i + 1)] = total[i:i + 1, :]

    all_rows.wait_send()
    for k in range(K):
        pair_copies(k).wait_send()
    for ring in (az, ax, bx, bz):
        ring.sent()
    up_other.wait_send()
    pltpu.make_async_remote_copy(src_ref=tokens.at[oc], dst_ref=other, send_sem=other_send, recv_sem=other_send,
                                 device_id=sibling, device_id_type=MESH).wait_send()


def body(tokens, up_panel):
    variants, depth, width = tokens.shape
    block, panel = up_panel.shape[1:]
    scale = 1.0 / (depth * lax.axis_size("tok"))
    dma = pltpu.SemaphoreType.DMA
    scratch = [
        pltpu.VMEM((depth, width), BF16),
        pltpu.VMEM((depth, width), BF16),
        pltpu.VMEM((WINDOW, 2 * depth), BF16),
        pltpu.VMEM((2, block, panel), BF16),
        pltpu.VMEM((NX, NZ, 2, WINDOW, 128), F32),
        pltpu.VMEM((UNIT, 128), F32),
        pltpu.VMEM((UNIT, 128), F32),
        pltpu.VMEM((UNIT, 128), F32),
        pltpu.VMEM((KA, 2, NX, UNIT, 128), F32),
        pltpu.VMEM((KB, 2, NZ, UNIT, 128), F32),
        pltpu.VMEM((K, 2, 2, UNIT, 128), F32),
        pltpu.VMEM((K, 2 * NY, 5, 8, 128), F32),
        pltpu.VMEM((K, 2 * NY - 1, 5, 8, 128), F32),
        pltpu.VMEM((K, 4, 8, 128), F32),
        pltpu.VMEM((CHIPS, 8, 128), F32),
        pltpu.VMEM((K, 8, 128), F32),
        dma((PIECES,)), dma, dma((PIECES,)), dma, dma, dma,
        dma((K,)), dma((K,)), dma, dma,
    ]
    for shape in SHAPES:
        scratch += Ring.scratch(*shape)
    gram, num = pl.pallas_call(
        functools.partial(kernel, scale),
        out_shape=(
            jax.ShapeDtypeStruct((WINDOW // NY, block), F32),
            jax.ShapeDtypeStruct((1, panel), F32),
        ),
        in_specs=[pl.BlockSpec(memory_space=pl.ANY)] * 2,
        out_specs=(pl.BlockSpec(memory_space=pltpu.VMEM),) * 2,
        scratch_shapes=scratch,
        compiler_params=pltpu.CompilerParams(
            collective_id=0, has_side_effects=True, vmem_limit_bytes=60 * 2**20
        ),
    )(tokens, up_panel)
    return gram, num


def solution(mesh):
    return jax.shard_map(
        body,
        mesh=mesh,
        in_specs=(P("var", "tok", None), P("var", "tok", None)),
        out_specs=(P("var", "tok"), P(("var", "tok"), None)),
        check_vma=False,
    )
```

```python
import functools

import jax
import jax.numpy as jnp
from jax import lax
from jax.experimental import pallas as pl
from jax.experimental.pallas import tpu as pltpu
from jax.sharding import PartitionSpec as P

WINDOW = 256
NX, NZ, NY = 4, 8, 4
CHIPS = NX * NZ
UNIT = 16
UNITS = WINDOW // UNIT
KA = 6
KB = UNITS - KA
PAIRS = UNITS // 2
POWER = 9
TOP = 2.0**13.8
MESH = pl.DeviceIdType.MESH
F32, BF16 = jnp.float32, jnp.bfloat16


def encode(value, factor):
    t = value * factor
    t2 = t * t
    t4 = t2 * t2
    return (t4 * t4 * t).astype(BF16)


def decode(code, factor):
    y = code.astype(F32)
    root = jnp.exp2(jnp.log(jnp.maximum(jnp.abs(y), 1e-38)) * (1.4426950408889634 / POWER))
    return jnp.where(y < 0, -root, root) * factor


class Ring:
    def __init__(self, n, blocks, units, me, device, base, source, refs):
        self.n, self.half, self.units = n, n // 2, units
        self.me, self.device, self.base, self.source = me, device, base, source
        (self.s0, self.sn, self.r0, self.rn, self.bs, self.br, self.enc, self.dec,
         self.send_sem, self.recv_sem, self.bsend_sem, self.brecv_sem) = refs

    @staticmethod
    def scratch(n, blocks, units):
        half = n // 2
        first = pltpu.VMEM((units, 2, blocks, UNIT, 128), BF16)
        later = pltpu.VMEM((units, 2, half - 1, 2, blocks, UNIT, 128), BF16)
        bound = pltpu.VMEM((2, half, UNIT, 128), F32)
        return [first, later, first, later, bound, bound, bound, bound,
                pltpu.SemaphoreType.DMA((2,)), pltpu.SemaphoreType.DMA((units, 2, half)),
                pltpu.SemaphoreType.DMA, pltpu.SemaphoreType.DMA((2, half))]

    def data_copy(self, k, d, s, to):
        if s == 0:
            src, dst = self.s0.at[k, d], self.r0.at[k, d]
        else:
            src, dst = self.sn.at[k, d, s - 1], self.rn.at[k, d, s - 1]
        return pltpu.make_async_remote_copy(
            src_ref=src, dst_ref=dst, send_sem=self.send_sem.at[min(s, 1)],
            recv_sem=self.recv_sem.at[k, d, s], device_id=to, device_id_type=MESH)

    def bound_copy(self, d, s, to):
        return pltpu.make_async_remote_copy(
            src_ref=self.bs.at[d, s], dst_ref=self.br.at[d, s], send_sem=self.bsend_sem,
            recv_sem=self.brecv_sem.at[d, s], device_id=to, device_id_type=MESH)

    def neighbour(self, d):
        return self.device(lax.rem(self.me + (1 if d == 0 else self.n - 1), self.n))

    def dest(self, d, s):
        far = self.half - s
        return lax.rem(self.me + (far if d == 0 else self.n - far), self.n)

    def bounds(self, s):
        for d in (0, 1):
            to = self.neighbour(d)
            bound = self.base[self.dest(d, s)]
            if s > 0:
                self.bound_copy(d, s - 1, to).wait_recv()
                came = self.br[d, s - 1]
                self.dec[d, s - 1] = came * (1.0 / TOP)
                bound = bound + came
            self.bs[d, s] = bound
            self.enc[d, s] = TOP / bound
            self.bound_copy(d, s, to).start()

    def send(self, s, k):
        for d in (0, 1):
            to = self.neighbour(d)
            dest = self.dest(d, s)
            enc = self.enc[d, s]
            if s == 0:
                self.s0[k, d] = encode(self.source(dest, d, k), enc)
            else:
                self.data_copy(k, d, s - 1, to).wait_recv()
                dec = self.dec[d, s - 1]
                for h in (0, 1):
                    value = self.source(dest, h, k)
                    if s > 1:
                        value = value + decode(self.rn[k, d, s - 2, h], dec)
                    elif h == d:
                        value = value + decode(self.r0[k, d], dec)
                    self.sn[k, d, s - 1, h] = encode(value, enc)
            self.data_copy(k, d, s, to).start()

    def last_bounds(self, total):
        last = self.half - 1
        for d in (0, 1):
            self.bound_copy(d, last, self.neighbour(d)).wait_recv()
            self.dec[d, last] = self.br[d, last] * (1.0 / TOP)
        total[...] = self.base[self.me] + self.br[0, last] + self.br[1, last]

    def finish(self, k, store):
        last = self.half - 1
        for d in (0, 1):
            self.data_copy(k, d, last, self.neighbour(d)).wait_recv()
        for h in (0, 1):
            value = self.source(self.me, h, k)
            for d in (0, 1):
                value = value + decode(self.rn[k, d, last - 1, h], self.dec[d, last])
            store(h, value)

    def sent(self):
        to = self.neighbour(0)
        for src, dst, sem in ((self.s0, self.r0, self.send_sem.at[0]), (self.sn, self.rn, self.send_sem.at[1]),
                              (self.bs, self.br, self.bsend_sem)):
            pltpu.make_async_remote_copy(src_ref=src, dst_ref=dst, send_sem=sem, recv_sem=sem,
                                         device_id=to, device_id_type=MESH).wait_send()


class Exchange:
    def __init__(self, n, units, me, device, mid, refs):
        self.n, self.units, self.me, self.device, self.mid = n, units, me, device, mid
        self.out, self.came, self.bound, self.bcame, self.send_sem, self.recv_sem, self.bsend_sem, self.brecv_sem = refs

    @staticmethod
    def scratch(n, units):
        return [pltpu.VMEM((units, n, 2, UNIT, 128), BF16), pltpu.VMEM((units, n - 1, 2, UNIT, 128), BF16),
                pltpu.VMEM((UNIT, 128), F32), pltpu.VMEM((n - 1, UNIT, 128), F32),
                pltpu.SemaphoreType.DMA((units,)), pltpu.SemaphoreType.DMA((units,)),
                pltpu.SemaphoreType.DMA, pltpu.SemaphoreType.DMA]

    def far(self, o):
        at = lax.rem(self.me + o, self.n)
        return at, self.device(at)

    def bounds(self):
        for o in range(1, self.n):
            pltpu.make_async_remote_copy(src_ref=self.bound, dst_ref=self.bcame.at[o - 1], send_sem=self.bsend_sem,
                                         recv_sem=self.brecv_sem, device_id=self.far(o)[1], device_id_type=MESH).start()

    def send(self, k):
        enc = TOP / self.bound[...]
        for h in (0, 1):
            self.out[k, :, h] = encode(self.mid[k, h], enc)
        for o in range(1, self.n):
            at, to = self.far(o)
            pltpu.make_async_remote_copy(src_ref=self.out.at[k, at], dst_ref=self.came.at[k, o - 1],
                                         send_sem=self.send_sem.at[k], recv_sem=self.recv_sem.at[k],
                                         device_id=to, device_id_type=MESH).start()

    def all_bounds(self):
        return pltpu.make_async_remote_copy(src_ref=self.bcame, dst_ref=self.bcame, send_sem=self.bsend_sem,
                                            recv_sem=self.brecv_sem, device_id=self.far(1)[1], device_id_type=MESH)

    def all_data(self, k):
        return pltpu.make_async_remote_copy(src_ref=self.came.at[k], dst_ref=self.came.at[k], send_sem=self.send_sem.at[k],
                                            recv_sem=self.recv_sem.at[k], device_id=self.far(1)[1], device_id_type=MESH)

    def finish(self, k, store):
        self.all_data(k).wait_recv()
        for h in (0, 1):
            value = self.mid[k, h, self.me]
            for o in range(self.n - 1):
                value = value + decode(self.came[k, o, h], self.bcame[o] * (1.0 / TOP))
            store(h, value)

    def sent(self):
        self.all_bounds().wait_send()
        for k in range(self.units):
            self.all_data(k).wait_send()


RINGS = ((NZ, NX, KA), (NX, NZ, KB))
EXCHANGES = ((NX, KA), (NZ, KB))


def kernel(scale, tokens, up, gram, num, own, other, wown, wother, wt, upv, prod, base_z, base_x, mid_a, mid_b, fin,
           msg1, recv1, msg2, recv2, gacc, own_sem, other_send, other_recv, up_sem, up_send, up_recv,
           send1, sem1, send2, sem2, met, *refs):
    y, t = lax.axis_index("var"), lax.axis_index("tok")
    c = lax.rem(t, 2)
    chip = t // 2
    z, x = lax.rem(chip, NZ), chip // NZ
    oc = 1 - c
    sibling = (y, chip * 2 + oc)
    depth = own.shape[0]
    along_z = lambda at: (y, (x * NZ + at) * 2 + c)
    along_x = lambda at: (y, (at * NZ + z) * 2 + c)
    rows = lambda u: pl.ds(pl.multiple_of(u * UNIT, UNIT), UNIT)

    parts = (
        (8, lambda i: (2, i)),
        (3, lambda i: (lax.rem(3 + i, 4), 4)),
        (6, lambda i: (lax.rem(3 + lax.rem(i, 3), 4), 3 + 2 * (i // 3))),
        (10, lambda i: (1 + 2 * (i // 5), lax.rem(6 + lax.rem(i, 5), 8))),
        (5, lambda i: (0, lax.rem(6 + i, 8))),
    )
    starts = [sum(p[0] for p in parts[:j]) for j in range(len(parts))]

    def block_at(part, i):
        dx, dz = parts[part][1](i)
        bx, bz = lax.rem(x + dx, NX), lax.rem(z + dz, NZ)
        return bx, bz, pl.ds(pl.multiple_of((bx * NZ + bz) * 256, 256), 256)

    def own_copy(cols, at):
        return pltpu.make_async_copy(tokens.at[c, :, cols], own.at[:, cols], own_sem.at[at])

    def other_copy(cols, at):
        return pltpu.make_async_remote_copy(
            src_ref=tokens.at[oc, :, cols], dst_ref=other.at[:, cols], send_sem=other_send,
            recv_sem=other_recv.at[at], device_id=sibling, device_id_type=MESH)

    def each_block(run):
        for part, (size, _) in enumerate(parts):
            def one(i, carry):
                run(block_at(part, i)[2], starts[part] + i)
                return carry
            lax.fori_loop(0, size, one, 0)

    front = pl.ds(0, WINDOW)
    wown_copy = pltpu.make_async_copy(tokens.at[c, :, front], wown, own_sem.at[CHIPS])
    wother_copy = pltpu.make_async_remote_copy(
        src_ref=tokens.at[oc, :, front], dst_ref=wother, send_sem=up_send.at[0], recv_sem=other_recv.at[CHIPS],
        device_id=sibling, device_id_type=MESH)
    up_own = pltpu.make_async_copy(up.at[c], upv.at[c], up_sem)
    up_other = pltpu.make_async_remote_copy(src_ref=up.at[oc], dst_ref=upv.at[c], send_sem=up_send.at[1],
                                            recv_sem=up_recv, device_id=sibling, device_id_type=MESH)

    barrier = pltpu.get_barrier_semaphore()
    peers = [sibling] + [along_z(lax.rem(z + o, NZ)) for o in (1, NZ - 1)]
    peers += [along_x(lax.rem(x + o, NX)) for o in (1, NX - 1)]
    over_y = [(lax.rem(y + o, NY), t) for o in range(1, NY)]
    for to in peers + over_y:
        pl.semaphore_signal(barrier, inc=1, device_id=to, device_id_type=MESH)
    wown_copy.start()
    each_block(lambda cols, at: own_copy(cols, at).start())
    up_own.start()

    row = lax.broadcasted_iota(jnp.int32, (WINDOW, WINDOW), 0)
    col = lax.broadcasted_iota(jnp.int32, (WINDOW, WINDOW), 1)
    feature = ((row >> 2) & 3) * (WINDOW // NY) + (row >> 4) * 4 + (row & 3)
    pick = jnp.where(col == feature, 1.0, 0.0).astype(BF16)

    def window(ref):
        return lax.dot_general(pick, ref[...], (((1,), (1,)), ((), ())), preferred_element_type=F32).astype(BF16)

    wown_copy.wait()
    wt[:, :depth] = window(wown)
    for ref in (base_z, base_x):
        ref[...] = jnp.full(ref.shape, 1e-33, F32)

    pl.semaphore_wait(barrier, len(peers) + len(over_y))
    wother_copy.start()
    each_block(lambda cols, at: other_copy(cols, at).start())
    up_other.start()
    for to in over_y:
        pl.semaphore_signal(met, inc=1, device_id=to, device_id_type=MESH)
    wother_copy.wait_recv()
    wt[:, depth:] = window(wother)

    def multiply(part):
        def one(i, carry):
            bx, bz, cols = block_at(part, i)
            at = starts[part] + i
            own_copy(cols, at).wait()
            other_copy(cols, at).wait_recv()
            product = jnp.dot(wt[:, :depth], own[:, cols], preferred_element_type=F32)
            product = product + jnp.dot(wt[:, depth:], other[:, cols], preferred_element_type=F32)
            prod[bx, bz, 0] = product[:, :128]
            prod[bx, bz, 1] = product[:, 128:]
            top = jnp.max(jnp.abs(product).reshape(UNITS, UNIT, 256), axis=0)
            top = jnp.maximum(top[:, :128], top[:, 128:])
            base_z[bz] = jnp.maximum(base_z[bz], top)
            base_x[bx] = jnp.maximum(base_x[bx], top)
            return carry
        lax.fori_loop(0, parts[part][0], one, 0)

    sizes = (12, 12, 8, 8)
    split = [refs[sum(sizes[:j]):sum(sizes[:j + 1])] for j in range(4)]
    az = Ring(*RINGS[0], z, along_z, base_z, lambda dest, h, k: prod[:, dest, h, rows(k), :], split[0])
    bx = Ring(*RINGS[1], x, along_x, base_x, lambda dest, h, k: prod[dest, :, h, rows(KA + k), :], split[1])
    ax = Exchange(*EXCHANGES[0], x, along_x, mid_a, split[2])
    bz = Exchange(*EXCHANGES[1], z, along_z, mid_b, split[3])

    def pair_of(o):
        pc = lax.rem(y * 2 + c + o, 2 * NY)
        return pc, (pc // 2, chip * 2 + lax.rem(pc, 2))

    def numerators(j):
        total = None
        for h in (0, 1):
            g = jnp.concatenate([fin[2 * j, h], fin[2 * j + 1, h]], axis=0)
            high = g.astype(BF16)
            low = (g - high.astype(F32)).astype(BF16)
            term = jnp.dot(jnp.concatenate([high, low], axis=0), upv[h], preferred_element_type=F32)
            total = term if total is None else total + term
        total = total[:2 * UNIT] + total[2 * UNIT:]
        tiles = total.reshape(2 * UNIT, 8, 128)
        for p in range(NY):
            for half in (0, 1):
                for ab in (0, 1):
                    for i in (0, 1):
                        msg1[j, 2 * p + half, 2 * ab + i] = tiles[UNIT * ab + 4 * p + 2 * i + half]
                    msg1[j, 2 * p + half, 4, 4 * ab:4 * ab + 4, :] = fin[2 * j + ab, half, 4 * p:4 * p + 4, :]

        def post(o, carry):
            pc, to = pair_of(o)
            pltpu.make_async_remote_copy(src_ref=msg1.at[j, pc], dst_ref=recv1.at[j, o - 1], send_sem=send1.at[j],
                                         recv_sem=sem1.at[j], device_id=to, device_id_type=MESH).start()
            return carry

        lax.fori_loop(1, 2 * NY, post, 0)

    def pair_copies(j):
        return pltpu.make_async_remote_copy(src_ref=recv1.at[j], dst_ref=recv1.at[j], send_sem=send1.at[j],
                                            recv_sem=sem1.at[j], device_id=sibling, device_id_type=MESH)

    def row_copy(src, to_chip):
        slot = lax.rem(to_chip - chip + CHIPS, CHIPS) - 1
        return pltpu.make_async_remote_copy(src_ref=src, dst_ref=recv2.at[slot], send_sem=send2, recv_sem=sem2,
                                            device_id=(y, to_chip * 2 + c), device_id_type=MESH)

    def pass_on(j):
        pair_copies(j).wait_recv()
        total = msg1[j, y * 2 + c]
        for o in range(2 * NY - 1):
            total = total + recv1[j, o]
        msg2[j] = total[:4]
        gacc[j] = total[4]

        def row_out(i, carry):
            u = 2 * j + i // 2
            to = (u // 4) * NZ + 2 * lax.rem(u, 4) + lax.rem(i, 2)

            @pl.when(to == chip)
            def _():
                recv2[CHIPS - 1] = msg2[j, i]

            @pl.when(to != chip)
            def _():
                row_copy(msg2.at[j, i], to).start()
            return carry

        lax.fori_loop(0, 4, row_out, 0)

    def run(step, low, high):
        def one(k, carry):
            step(k)
            return carry
        lax.fori_loop(low, high, one, 0)

    def put(ref, k):
        def store(h, value):
            ref[k, h] = value
        return store

    def put_final(u):
        def store(h, value):
            fin[u, h] = value * scale
        return store

    def a_turn(k):
        az.finish(k, put(mid_a, k))
        ax.send(k)

    def b_turn(k):
        bx.finish(k, put(mid_b, k))
        bz.send(k)

    def a_pair(j):
        for i in (0, 1):
            ax.finish(2 * j + i, put_final(2 * j + i))
        numerators(j)

    def b_pair(j):
        for i in (0, 1):
            bz.finish(2 * j + i, put_final(KA + 2 * j + i))
        numerators(KA // 2 + j)

    a_send = lambda s: functools.partial(az.send, s)
    b_send = lambda s: functools.partial(bx.send, s)
    half_b = KB // 2
    multiply(0)
    multiply(1)
    az.bounds(0)
    run(a_send(0), 0, KA)
    bx.bounds(0)
    run(b_send(0), 0, KB)
    multiply(2)
    az.bounds(1)
    run(a_send(1), 0, KA)
    multiply(3)
    bx.bounds(1)
    run(b_send(1), 0, half_b)
    multiply(4)
    az.bounds(2)
    run(a_send(2), 0, KA)
    run(b_send(1), half_b, KB)
    az.bounds(3)
    run(a_send(3), 0, KA)
    bx.last_bounds(bz.bound)
    az.last_bounds(ax.bound)
    bz.bounds()
    ax.bounds()
    run(b_turn, 0, 3)
    run(a_turn, 0, KA)
    run(b_turn, 3, KB - 3)
    up_own.wait()
    up_other.wait_recv()
    pl.semaphore_wait(met, NY - 1)
    ax.all_bounds().wait_recv()
    run(a_pair, 0, KA // 2)
    run(b_turn, KB - 3, KB)
    bz.all_bounds().wait_recv()
    run(pass_on, 0, KA // 2)
    b_pair(0)

    def b_step(j):
        b_pair(j)
        pass_on(KA // 2 + j - 1)

    run(b_step, 1, KB // 2)
    pass_on(PAIRS - 1)

    for u in range(UNITS):
        gram[4 * u:4 * u + 4, :] = gacc[u // 2, 4 * (u % 2):4 * (u % 2) + 4, :]
    all_rows = pltpu.make_async_remote_copy(src_ref=recv2.at[pl.ds(0, CHIPS - 1)], dst_ref=recv2.at[pl.ds(0, CHIPS - 1)],
                                            send_sem=send2, recv_sem=sem2, device_id=sibling, device_id_type=MESH)
    all_rows.wait_send()
    for j in range(PAIRS):
        pair_copies(j).wait_send()
    for group in (az, bx, ax, bz):
        group.sent()
    wother_copy.wait_send()
    up_other.wait_send()
    pltpu.make_async_remote_copy(src_ref=tokens.at[oc], dst_ref=other, send_sem=other_send, recv_sem=other_send,
                                 device_id=sibling, device_id_type=MESH).wait_send()
    all_rows.wait_recv()
    total = jnp.sum(recv2[...], axis=0)
    for i in range(8):
        num[0:1, 128 * i:128 * (i + 1)] = total[i:i + 1, :]


def body(tokens, up_panel):
    variants, depth, width = tokens.shape
    block, panel = up_panel.shape[1:]
    scale = 1.0 / (depth * lax.axis_size("tok"))
    dma = pltpu.SemaphoreType.DMA
    scratch = [
        pltpu.VMEM((depth, width), BF16),
        pltpu.VMEM((depth, width), BF16),
        pltpu.VMEM((depth, WINDOW), BF16),
        pltpu.VMEM((depth, WINDOW), BF16),
        pltpu.VMEM((WINDOW, 2 * depth), BF16),
        pltpu.VMEM((2, block, panel), BF16),
        pltpu.VMEM((NX, NZ, 2, WINDOW, 128), F32),
        pltpu.VMEM((NZ, UNIT, 128), F32),
        pltpu.VMEM((NX, UNIT, 128), F32),
        pltpu.VMEM((KA, 2, NX, UNIT, 128), F32),
        pltpu.VMEM((KB, 2, NZ, UNIT, 128), F32),
        pltpu.VMEM((UNITS, 2, UNIT, 128), F32),
        pltpu.VMEM((PAIRS, 2 * NY, 5, 8, 128), F32),
        pltpu.VMEM((PAIRS, 2 * NY - 1, 5, 8, 128), F32),
        pltpu.VMEM((PAIRS, 4, 8, 128), F32),
        pltpu.VMEM((CHIPS, 8, 128), F32),
        pltpu.VMEM((PAIRS, 8, 128), F32),
        dma((CHIPS + 1,)), dma, dma((CHIPS + 1,)), dma, dma((2,)), dma,
        dma((PAIRS,)), dma((PAIRS,)), dma, dma, pltpu.SemaphoreType.REGULAR,
    ]
    for shape in RINGS:
        scratch += Ring.scratch(*shape)
    for shape in EXCHANGES:
        scratch += Exchange.scratch(*shape)
    gram, num = pl.pallas_call(
        functools.partial(kernel, scale),
        out_shape=(
            jax.ShapeDtypeStruct((WINDOW // NY, block), F32),
            jax.ShapeDtypeStruct((1, panel), F32),
        ),
        in_specs=[pl.BlockSpec(memory_space=pl.ANY)] * 2,
        out_specs=(pl.BlockSpec(memory_space=pltpu.VMEM),) * 2,
        scratch_shapes=scratch,
        compiler_params=pltpu.CompilerParams(
            collective_id=0, has_side_effects=True, vmem_limit_bytes=60 * 2**20
        ),
    )(tokens, up_panel)
    return gram, num


def solution(mesh):
    return jax.shard_map(
        body,
        mesh=mesh,
        in_specs=(P("var", "tok", None), P("var", "tok", None)),
        out_specs=(P("var", "tok"), P(("var", "tok"), None)),
        check_vma=False,
    )
```

```python
import functools

import jax
import jax.numpy as jnp
from jax import lax
from jax.experimental import pallas as pl
from jax.experimental.pallas import tpu as pltpu
from jax.sharding import PartitionSpec as P

WINDOW = 256
NX, NZ, NY = 4, 8, 4
CHIPS = NX * NZ
UNIT = 16
UNITS = WINDOW // UNIT
KA = 6
KB = UNITS - KA
PAIRS = UNITS // 2
A2, A3, AT, BT, BE, AP, BP = 1, 5, 9, 5, 7, 14, 11
POWER = 9
TOP = 2.0**13.8
MESH = pl.DeviceIdType.MESH
F32, BF16 = jnp.float32, jnp.bfloat16


def encode(value, factor):
    t = value * factor
    t2 = t * t
    t4 = t2 * t2
    return (t4 * t4 * t).astype(BF16)


def decode(code, factor):
    y = code.astype(F32)
    root = jnp.exp2(jnp.log(jnp.maximum(jnp.abs(y), 1e-38)) * (1.4426950408889634 / POWER))
    return jnp.where(y < 0, -root, root) * factor


class Ring:
    def __init__(self, n, blocks, units, me, device, base, source, refs):
        self.n, self.half, self.units = n, n // 2, units
        self.me, self.device, self.base, self.source = me, device, base, source
        (self.s0, self.sn, self.r0, self.rn, self.bs, self.br, self.enc, self.dec,
         self.send_sem, self.recv_sem, self.bsend_sem, self.brecv_sem) = refs

    @staticmethod
    def scratch(n, blocks, units):
        half = n // 2
        first = pltpu.VMEM((units, 2, blocks, UNIT, 128), BF16)
        later = pltpu.VMEM((units, 2, half - 1, 2, blocks, UNIT, 128), BF16)
        bound = pltpu.VMEM((2, half, UNIT, 128), F32)
        return [first, later, first, later, bound, bound, bound, bound,
                pltpu.SemaphoreType.DMA((2,)), pltpu.SemaphoreType.DMA((units, 2, half)),
                pltpu.SemaphoreType.DMA, pltpu.SemaphoreType.DMA((2, half))]

    def data_copy(self, k, d, s, to):
        if s == 0:
            src, dst = self.s0.at[k, d], self.r0.at[k, d]
        else:
            src, dst = self.sn.at[k, d, s - 1], self.rn.at[k, d, s - 1]
        return pltpu.make_async_remote_copy(
            src_ref=src, dst_ref=dst, send_sem=self.send_sem.at[min(s, 1)],
            recv_sem=self.recv_sem.at[k, d, s], device_id=to, device_id_type=MESH)

    def bound_copy(self, d, s, to):
        return pltpu.make_async_remote_copy(
            src_ref=self.bs.at[d, s], dst_ref=self.br.at[d, s], send_sem=self.bsend_sem,
            recv_sem=self.brecv_sem.at[d, s], device_id=to, device_id_type=MESH)

    def neighbour(self, d):
        return self.device(lax.rem(self.me + (1 if d == 0 else self.n - 1), self.n))

    def dest(self, d, s):
        far = self.half - s
        return lax.rem(self.me + (far if d == 0 else self.n - far), self.n)

    def bounds(self, s):
        for d in (0, 1):
            to = self.neighbour(d)
            bound = self.base[self.dest(d, s)]
            if s > 0:
                self.bound_copy(d, s - 1, to).wait_recv()
                came = self.br[d, s - 1]
                self.dec[d, s - 1] = came * (1.0 / TOP)
                bound = bound + came
            self.bs[d, s] = bound
            self.enc[d, s] = TOP / bound
            self.bound_copy(d, s, to).start()

    def send(self, s, k):
        for d in (0, 1):
            to = self.neighbour(d)
            dest = self.dest(d, s)
            enc = self.enc[d, s]
            if s == 0:
                self.s0[k, d] = encode(self.source(dest, d, k), enc)
            else:
                self.data_copy(k, d, s - 1, to).wait_recv()
                dec = self.dec[d, s - 1]
                for h in (0, 1):
                    value = self.source(dest, h, k)
                    if s > 1:
                        value = value + decode(self.rn[k, d, s - 2, h], dec)
                    elif h == d:
                        value = value + decode(self.r0[k, d], dec)
                    self.sn[k, d, s - 1, h] = encode(value, enc)
            self.data_copy(k, d, s, to).start()

    def last_bounds(self, total):
        last = self.half - 1
        for d in (0, 1):
            self.bound_copy(d, last, self.neighbour(d)).wait_recv()
            self.dec[d, last] = self.br[d, last] * (1.0 / TOP)
        total[...] = self.base[self.me] + self.br[0, last] + self.br[1, last]

    def finish(self, k, store):
        last = self.half - 1
        for d in (0, 1):
            self.data_copy(k, d, last, self.neighbour(d)).wait_recv()
        for h in (0, 1):
            value = self.source(self.me, h, k)
            for d in (0, 1):
                value = value + decode(self.rn[k, d, last - 1, h], self.dec[d, last])
            store(h, value)

    def sent(self):
        to = self.neighbour(0)
        for src, dst, sem in ((self.s0, self.r0, self.send_sem.at[0]), (self.sn, self.rn, self.send_sem.at[1]),
                              (self.bs, self.br, self.bsend_sem)):
            pltpu.make_async_remote_copy(src_ref=src, dst_ref=dst, send_sem=sem, recv_sem=sem,
                                         device_id=to, device_id_type=MESH).wait_send()


class Exchange:
    def __init__(self, n, units, me, device, mid, refs):
        self.n, self.units, self.me, self.device, self.mid = n, units, me, device, mid
        self.out, self.came, self.bound, self.bcame, self.send_sem, self.recv_sem, self.bsend_sem, self.brecv_sem = refs

    @staticmethod
    def scratch(n, units):
        return [pltpu.VMEM((units, n, 2, UNIT, 128), BF16), pltpu.VMEM((units, n - 1, 2, UNIT, 128), BF16),
                pltpu.VMEM((UNIT, 128), F32), pltpu.VMEM((n - 1, UNIT, 128), F32),
                pltpu.SemaphoreType.DMA((units,)), pltpu.SemaphoreType.DMA((units,)),
                pltpu.SemaphoreType.DMA, pltpu.SemaphoreType.DMA]

    def far(self, o):
        at = lax.rem(self.me + o, self.n)
        return at, self.device(at)

    def bounds(self):
        for o in range(1, self.n):
            pltpu.make_async_remote_copy(src_ref=self.bound, dst_ref=self.bcame.at[o - 1], send_sem=self.bsend_sem,
                                         recv_sem=self.brecv_sem, device_id=self.far(o)[1], device_id_type=MESH).start()

    def send(self, k):
        enc = TOP / self.bound[...]
        for h in (0, 1):
            self.out[k, :, h] = encode(self.mid[k, h], enc)
        for o in range(1, self.n):
            at, to = self.far(o)
            pltpu.make_async_remote_copy(src_ref=self.out.at[k, at], dst_ref=self.came.at[k, o - 1],
                                         send_sem=self.send_sem.at[k], recv_sem=self.recv_sem.at[k],
                                         device_id=to, device_id_type=MESH).start()

    def all_bounds(self):
        return pltpu.make_async_remote_copy(src_ref=self.bcame, dst_ref=self.bcame, send_sem=self.bsend_sem,
                                            recv_sem=self.brecv_sem, device_id=self.far(1)[1], device_id_type=MESH)

    def all_data(self, k):
        return pltpu.make_async_remote_copy(src_ref=self.came.at[k], dst_ref=self.came.at[k], send_sem=self.send_sem.at[k],
                                            recv_sem=self.recv_sem.at[k], device_id=self.far(1)[1], device_id_type=MESH)

    def finish(self, k, store):
        self.all_data(k).wait_recv()
        for h in (0, 1):
            value = self.mid[k, h, self.me]
            for o in range(self.n - 1):
                value = value + decode(self.came[k, o, h], self.bcame[o] * (1.0 / TOP))
            store(h, value)

    def sent(self):
        self.all_bounds().wait_send()
        for k in range(self.units):
            self.all_data(k).wait_send()


class HalfExchange(Exchange):
    def __init__(self, n, units, me, device, mid, refs):
        super().__init__(n, units, me, device, mid, refs[:8])
        self.half = n // 2
        self.pre, self.got, self.near, self.total, self.pre_send, self.pre_recv, self.near_send, self.near_recv = refs[8:]
        self.others = [o for o in range(1, n) if o != self.half]

    @staticmethod
    def scratch(n, units):
        dma = pltpu.SemaphoreType.DMA
        piece = pltpu.VMEM((units, 2, UNIT, 128), BF16)
        return [pltpu.VMEM((units, n, 2, UNIT, 128), BF16), pltpu.VMEM((units, n - 2, 2, UNIT, 128), BF16),
                pltpu.VMEM((UNIT, 128), F32), pltpu.VMEM((n - 2, UNIT, 128), F32),
                dma((units,)), dma((units,)), dma, dma,
                piece, piece, pltpu.VMEM((2, UNIT, 128), F32), pltpu.VMEM((UNIT, 128), F32),
                dma, dma((units, 2)), dma, dma((2,))]

    def near_copy(self, d):
        to = self.far(1 if d == 0 else self.n - 1)[1]
        return pltpu.make_async_remote_copy(src_ref=self.bound, dst_ref=self.near.at[d], send_sem=self.near_send,
                                            recv_sem=self.near_recv.at[d], device_id=to, device_id_type=MESH)

    def pre_copy(self, k, d):
        to = self.far(1 if d == 0 else self.n - 1)[1]
        return pltpu.make_async_remote_copy(src_ref=self.pre.at[k, d], dst_ref=self.got.at[k, d], send_sem=self.pre_send,
                                            recv_sem=self.pre_recv.at[k, d], device_id=to, device_id_type=MESH)

    def near_bounds(self):
        for d in (0, 1):
            self.near_copy(d).start()

    def first(self, k):
        enc = TOP / self.bound[...]
        for d in (0, 1):
            self.pre[k, d] = encode(self.mid[k, d, self.far(self.half)[0]], enc)
            self.pre_copy(k, d).start()

    def bounds(self):
        for d in (0, 1):
            self.near_copy(d).wait_recv()
        self.total[...] = self.bound[...] + self.near[0] + self.near[1]
        for slot, o in enumerate(self.others):
            pltpu.make_async_remote_copy(src_ref=self.total, dst_ref=self.bcame.at[slot], send_sem=self.bsend_sem,
                                         recv_sem=self.brecv_sem, device_id=self.far(o)[1], device_id_type=MESH).start()

    def send(self, k):
        for d in (0, 1):
            self.pre_copy(k, d).wait_recv()
            at = self.far(self.half - 1 if d == 0 else self.half + 1)[0]
            self.mid[k, d, at] = self.mid[k, d, at] + decode(self.got[k, d], self.near[d] * (1.0 / TOP))
        enc = TOP / self.total[...]
        for h in (0, 1):
            self.out[k, :, h] = encode(self.mid[k, h], enc)
        for slot, o in enumerate(self.others):
            at, to = self.far(o)
            pltpu.make_async_remote_copy(src_ref=self.out.at[k, at], dst_ref=self.came.at[k, slot],
                                         send_sem=self.send_sem.at[k], recv_sem=self.recv_sem.at[k],
                                         device_id=to, device_id_type=MESH).start()

    def finish(self, k, store):
        self.all_data(k).wait_recv()
        for h in (0, 1):
            value = self.mid[k, h, self.me]
            for slot in range(self.n - 2):
                value = value + decode(self.came[k, slot, h], self.bcame[slot] * (1.0 / TOP))
            store(h, value)

    def sent(self):
        super().sent()
        to = self.far(1)[1]
        for src, dst, sem in ((self.pre, self.got, self.pre_send), (self.near, self.near, self.near_send)):
            pltpu.make_async_remote_copy(src_ref=src, dst_ref=dst, send_sem=sem, recv_sem=sem,
                                         device_id=to, device_id_type=MESH).wait_send()


RINGS = ((NZ, NX, KA), (NX, NZ, KB))
EXCHANGES = ((NX, KA), (NZ, KB))


def kernel(scale, tokens, up, gram, num, own, other, wown, wother, wt, upv, prod, base_z, base_x, mid_a, mid_b, fin,
           msg1, joined, recv1, msg2, recv2, gacc, own_sem, other_send, other_recv, up_sem, up_send, up_recv,
           send0, sem0, send1, sem1, send2, sem2, *refs):
    y, t = lax.axis_index("var"), lax.axis_index("tok")
    c = lax.rem(t, 2)
    chip = t // 2
    z, x = lax.rem(chip, NZ), chip // NZ
    oc = 1 - c
    sibling = (y, chip * 2 + oc)
    depth = own.shape[0]
    along_z = lambda at: (y, (x * NZ + at) * 2 + c)
    along_x = lambda at: (y, (at * NZ + z) * 2 + c)
    rows = lambda u: pl.ds(pl.multiple_of(u * UNIT, UNIT), UNIT)

    parts = (
        (8, lambda i: (2, i)),
        (3, lambda i: (lax.rem(3 + i, 4), 4)),
        (6, lambda i: (lax.rem(3 + lax.rem(i, 3), 4), 3 + 2 * (i // 3))),
        (10, lambda i: (1 + 2 * (i // 5), lax.rem(6 + lax.rem(i, 5), 8))),
        (5, lambda i: (0, lax.rem(6 + i, 8))),
    )
    starts = [sum(p[0] for p in parts[:j]) for j in range(len(parts))]

    def block_at(part, i):
        dx, dz = parts[part][1](i)
        bx, bz = lax.rem(x + dx, NX), lax.rem(z + dz, NZ)
        return bx, bz, pl.ds(pl.multiple_of((bx * NZ + bz) * 256, 256), 256)

    def own_copy(cols, at):
        return pltpu.make_async_copy(tokens.at[c, :, cols], own.at[:, cols], own_sem.at[at])

    def other_copy(cols, at):
        return pltpu.make_async_remote_copy(
            src_ref=tokens.at[oc, :, cols], dst_ref=other.at[:, cols], send_sem=other_send,
            recv_sem=other_recv.at[at], device_id=sibling, device_id_type=MESH)

    def each_block(run):
        for part, (size, _) in enumerate(parts):
            def one(i, carry):
                run(block_at(part, i)[2], starts[part] + i)
                return carry
            lax.fori_loop(0, size, one, 0)

    front = pl.ds(0, WINDOW)
    wown_copy = pltpu.make_async_copy(tokens.at[c, :, front], wown, own_sem.at[CHIPS])
    wother_copy = pltpu.make_async_remote_copy(
        src_ref=tokens.at[oc, :, front], dst_ref=wother, send_sem=up_send.at[0], recv_sem=other_recv.at[CHIPS],
        device_id=sibling, device_id_type=MESH)
    up_own = pltpu.make_async_copy(up.at[c], upv.at[c], up_sem)
    up_other = pltpu.make_async_remote_copy(src_ref=up.at[oc], dst_ref=upv.at[c], send_sem=up_send.at[1],
                                            recv_sem=up_recv, device_id=sibling, device_id_type=MESH)

    barrier = pltpu.get_barrier_semaphore()
    peers = [sibling] + [along_z(lax.rem(z + o, NZ)) for o in (1, NZ - 1)]
    peers += [along_x(lax.rem(x + o, NX)) for o in (1, NX - 1)]
    over_y = [(lax.rem(y + o, NY), t) for o in range(1, NY)]
    for to in peers + over_y:
        pl.semaphore_signal(barrier, inc=1, device_id=to, device_id_type=MESH)
    wown_copy.start()
    each_block(lambda cols, at: own_copy(cols, at).start())
    up_own.start()

    row = lax.broadcasted_iota(jnp.int32, (WINDOW, WINDOW), 0)
    col = lax.broadcasted_iota(jnp.int32, (WINDOW, WINDOW), 1)
    feature = ((row >> 2) & 3) * (WINDOW // NY) + (row >> 4) * 4 + (row & 3)
    pick = jnp.where(col == feature, 1.0, 0.0).astype(BF16)

    def window(ref):
        return lax.dot_general(pick, ref[...], (((1,), (1,)), ((), ())), preferred_element_type=F32).astype(BF16)

    wown_copy.wait()
    wt[:, :depth] = window(wown)
    for ref in (base_z, base_x):
        ref[...] = jnp.full(ref.shape, 1e-33, F32)

    pl.semaphore_wait(barrier, len(peers) + len(over_y))
    wother_copy.start()
    each_block(lambda cols, at: other_copy(cols, at).start())
    up_other.start()
    wother_copy.wait_recv()
    wt[:, depth:] = window(wother)

    def multiply(part):
        def one(i, carry):
            bx, bz, cols = block_at(part, i)
            at = starts[part] + i
            own_copy(cols, at).wait()
            other_copy(cols, at).wait_recv()
            product = jnp.dot(wt[:, :depth], own[:, cols], preferred_element_type=F32)
            product = product + jnp.dot(wt[:, depth:], other[:, cols], preferred_element_type=F32)
            prod[bx, bz, 0] = product[:, :128]
            prod[bx, bz, 1] = product[:, 128:]
            top = jnp.max(jnp.abs(product).reshape(UNITS, UNIT, 256), axis=0)
            top = jnp.maximum(top[:, :128], top[:, 128:])
            base_z[bz] = jnp.maximum(base_z[bz], top)
            base_x[bx] = jnp.maximum(base_x[bx], top)
            return carry
        lax.fori_loop(0, parts[part][0], one, 0)

    sizes = (12, 12, 8, 16)
    split = [refs[sum(sizes[:j]):sum(sizes[:j + 1])] for j in range(4)]
    az = Ring(*RINGS[0], z, along_z, base_z, lambda dest, h, k: prod[:, dest, h, rows(k), :], split[0])
    bx = Ring(*RINGS[1], x, along_x, base_x, lambda dest, h, k: prod[dest, :, h, rows(KA + k), :], split[1])
    ax = Exchange(*EXCHANGES[0], x, along_x, mid_a, split[2])
    bz = HalfExchange(*EXCHANGES[1], z, along_z, mid_b, split[3])

    def numerators(j):
        total = None
        for h in (0, 1):
            g = jnp.concatenate([fin[2 * j, h], fin[2 * j + 1, h]], axis=0)
            high = g.astype(BF16)
            low = (g - high.astype(F32)).astype(BF16)
            term = jnp.dot(jnp.concatenate([high, low], axis=0), upv[h], preferred_element_type=F32)
            total = term if total is None else total + term
        total = total[:2 * UNIT] + total[2 * UNIT:]
        tiles = total.reshape(2 * UNIT, 8, 128)
        for p in range(NY):
            for half in (0, 1):
                for ab in (0, 1):
                    for i in (0, 1):
                        msg1[j, half, p, 2 * ab + i] = tiles[UNIT * ab + 4 * p + 2 * i + half]
                    msg1[j, half, p, 4, 4 * ab:4 * ab + 4, :] = fin[2 * j + ab, half, 4 * p:4 * p + 4, :]
        core_copy(j).start()

    def core_copy(j):
        return pltpu.make_async_remote_copy(src_ref=msg1.at[j, oc], dst_ref=joined.at[j], send_sem=send0.at[j],
                                            recv_sem=sem0.at[j], device_id=sibling, device_id_type=MESH)

    def join(j):
        core_copy(j).wait_recv()
        for p in range(NY):
            msg1[j, c, p] = msg1[j, c, p] + joined[j, p]
        for o in range(1, NY):
            p = lax.rem(y + o, NY)
            pltpu.make_async_remote_copy(src_ref=msg1.at[j, c, p], dst_ref=recv1.at[j, o - 1], send_sem=send1.at[j],
                                         recv_sem=sem1.at[j], device_id=(p, t), device_id_type=MESH).start()

    def pair_copies(j):
        return pltpu.make_async_remote_copy(src_ref=recv1.at[j], dst_ref=recv1.at[j], send_sem=send1.at[j],
                                            recv_sem=sem1.at[j], device_id=sibling, device_id_type=MESH)

    def row_copy(src, to_chip):
        slot = lax.rem(to_chip - chip + CHIPS, CHIPS) - 1
        return pltpu.make_async_remote_copy(src_ref=src, dst_ref=recv2.at[slot], send_sem=send2, recv_sem=sem2,
                                            device_id=(y, to_chip * 2 + c), device_id_type=MESH)

    def pass_on(j):
        pair_copies(j).wait_recv()
        total = msg1[j, c, y]
        for o in range(NY - 1):
            total = total + recv1[j, o]
        msg2[j] = total[:4]
        gacc[j] = total[4]

        def row_out(i, carry):
            u = 2 * j + i // 2
            to = (u // 4) * NZ + 2 * lax.rem(u, 4) + lax.rem(i, 2)

            @pl.when(to == chip)
            def _():
                recv2[CHIPS - 1] = msg2[j, i]

            @pl.when(to != chip)
            def _():
                row_copy(msg2.at[j, i], to).start()
            return carry

        lax.fori_loop(0, 4, row_out, 0)

    def run(step, low, high):
        def one(k, carry):
            step(k)
            return carry
        lax.fori_loop(low, high, one, 0)

    def put(ref, k):
        def store(h, value):
            ref[k, h] = value
        return store

    def put_final(u):
        def store(h, value):
            fin[u, h] = value * scale
        return store

    def a_turn(k):
        az.finish(k, put(mid_a, k))
        ax.send(k)

    def b_turn(k):
        bx.finish(k, put(mid_b, k))
        bz.first(k)

    def a_pair(j):
        for i in (0, 1):
            ax.finish(2 * j + i, put_final(2 * j + i))
        numerators(j)

    def b_pair(j):
        for i in (0, 1):
            bz.finish(2 * j + i, put_final(KA + 2 * j + i))
        numerators(KA // 2 + j)

    def at_tick(at, start, count, step, prepare=None):
        def now():
            if prepare is not None:
                pl.when(at == start)(prepare)
            step(at - start)
        pl.when(jnp.logical_and(at >= start, at < start + count))(now)

    def two(step):
        return lambda m: run(step, 2 * m, 2 * m + 2)

    def every_other(step):
        return lambda m: pl.when(lax.rem(m, 2) == 0)(lambda: step(m // 2))

    a_send = lambda s: functools.partial(az.send, s)
    b_send = lambda s: functools.partial(bx.send, s)
    half_a, half_b = KA // 2, KB // 2

    def a_meet():
        az.last_bounds(ax.bound)
        ax.bounds()

    def b_meet():
        bx.last_bounds(bz.bound)
        bz.near_bounds()

    multiply(0)
    multiply(1)
    az.bounds(0)
    run(a_send(0), 0, KA)
    bx.bounds(0)
    run(b_send(0), 0, KB)
    multiply(2)
    az.bounds(1)
    run(a_send(1), 0, KA)
    multiply(3)
    bx.bounds(1)
    b_send(1)(0)
    multiply(4)
    up_own.wait()
    up_other.wait_recv()

    def tick(at, carry):
        at_tick(at, A2, half_a, two(a_send(2)), lambda: az.bounds(2))
        at_tick(at, A3, half_a, two(a_send(3)), lambda: az.bounds(3))
        at_tick(at, 1, KB - 1, lambda k: bx.send(1, k + 1))
        at_tick(at, AT, half_a, two(a_turn), a_meet)
        at_tick(at, BT, KB, b_turn, b_meet)
        at_tick(at, BE, KB, bz.send, bz.bounds)
        at_tick(at, AP, half_a, a_pair, lambda: ax.all_bounds().wait_recv())
        at_tick(at, BP, KB - 1, every_other(b_pair), lambda: bz.all_bounds().wait_recv())
        at_tick(at, AP + 1, half_a, join)
        at_tick(at, BP + 1, KB - 1, every_other(lambda j: join(half_a + j)))
        return carry

    lax.fori_loop(0, BP + KB, tick, 0)
    run(pass_on, 0, PAIRS)

    for u in range(UNITS):
        gram[4 * u:4 * u + 4, :] = gacc[u // 2, 4 * (u % 2):4 * (u % 2) + 4, :]
    all_rows = pltpu.make_async_remote_copy(src_ref=recv2.at[pl.ds(0, CHIPS - 1)], dst_ref=recv2.at[pl.ds(0, CHIPS - 1)],
                                            send_sem=send2, recv_sem=sem2, device_id=sibling, device_id_type=MESH)
    all_rows.wait_send()
    for j in range(PAIRS):
        pair_copies(j).wait_send()
        core_copy(j).wait_send()
    for group in (az, bx, ax, bz):
        group.sent()
    wother_copy.wait_send()
    up_other.wait_send()
    pltpu.make_async_remote_copy(src_ref=tokens.at[oc], dst_ref=other, send_sem=other_send, recv_sem=other_send,
                                 device_id=sibling, device_id_type=MESH).wait_send()
    all_rows.wait_recv()
    total = jnp.sum(recv2[...], axis=0)
    for i in range(8):
        num[0:1, 128 * i:128 * (i + 1)] = total[i:i + 1, :]


def body(tokens, up_panel):
    variants, depth, width = tokens.shape
    block, panel = up_panel.shape[1:]
    scale = 1.0 / (depth * lax.axis_size("tok"))
    dma = pltpu.SemaphoreType.DMA
    scratch = [
        pltpu.VMEM((depth, width), BF16),
        pltpu.VMEM((depth, width), BF16),
        pltpu.VMEM((depth, WINDOW), BF16),
        pltpu.VMEM((depth, WINDOW), BF16),
        pltpu.VMEM((WINDOW, 2 * depth), BF16),
        pltpu.VMEM((2, block, panel), BF16),
        pltpu.VMEM((NX, NZ, 2, WINDOW, 128), F32),
        pltpu.VMEM((NZ, UNIT, 128), F32),
        pltpu.VMEM((NX, UNIT, 128), F32),
        pltpu.VMEM((KA, 2, NX, UNIT, 128), F32),
        pltpu.VMEM((KB, 2, NZ, UNIT, 128), F32),
        pltpu.VMEM((UNITS, 2, UNIT, 128), F32),
        pltpu.VMEM((PAIRS, 2, NY, 5, 8, 128), F32),
        pltpu.VMEM((PAIRS, NY, 5, 8, 128), F32),
        pltpu.VMEM((PAIRS, NY - 1, 5, 8, 128), F32),
        pltpu.VMEM((PAIRS, 4, 8, 128), F32),
        pltpu.VMEM((CHIPS, 8, 128), F32),
        pltpu.VMEM((PAIRS, 8, 128), F32),
        dma((CHIPS + 1,)), dma, dma((CHIPS + 1,)), dma, dma((2,)), dma,
        dma((PAIRS,)), dma((PAIRS,)), dma((PAIRS,)), dma((PAIRS,)), dma, dma,
    ]
    for shape in RINGS:
        scratch += Ring.scratch(*shape)
    scratch += Exchange.scratch(*EXCHANGES[0]) + HalfExchange.scratch(*EXCHANGES[1])
    gram, num = pl.pallas_call(
        functools.partial(kernel, scale),
        out_shape=(
            jax.ShapeDtypeStruct((WINDOW // NY, block), F32),
            jax.ShapeDtypeStruct((1, panel), F32),
        ),
        in_specs=[pl.BlockSpec(memory_space=pl.ANY)] * 2,
        out_specs=(pl.BlockSpec(memory_space=pltpu.VMEM),) * 2,
        scratch_shapes=scratch,
        compiler_params=pltpu.CompilerParams(
            collective_id=0, has_side_effects=True, vmem_limit_bytes=60 * 2**20
        ),
    )(tokens, up_panel)
    return gram, num


def solution(mesh):
    return jax.shard_map(
        body,
        mesh=mesh,
        in_specs=(P("var", "tok", None), P("var", "tok", None)),
        out_specs=(P("var", "tok"), P(("var", "tok"), None)),
        check_vma=False,
    )
```

```python
import functools

import jax
import jax.numpy as jnp
from jax import lax
from jax.experimental import pallas as pl
from jax.experimental.pallas import tpu as pltpu
from jax.sharding import PartitionSpec as P

WINDOW = 256
NX, NZ, NY = 4, 8, 4
CHIPS = NX * NZ
UNIT = 16
UNITS = WINDOW // UNIT
KA = 6
KB = UNITS - KA
PAIRS = UNITS // 2
A2, A3, AT, BT, BE, AP, BP = 1, 4, 10, 3, 6, 14, 11
POWER = 9
TOP = 2.0**13.8
MESH = pl.DeviceIdType.MESH
F32, BF16 = jnp.float32, jnp.bfloat16


def encode(value, factor):
    t = value * factor
    t2 = t * t
    t4 = t2 * t2
    return (t4 * t4 * t).astype(BF16)


def decode(code, factor):
    y = code.astype(F32)
    root = jnp.exp2(jnp.log(jnp.maximum(jnp.abs(y), 1e-38)) * (1.4426950408889634 / POWER))
    return jnp.where(y < 0, -root, root) * factor


class Ring:
    def __init__(self, n, blocks, units, me, device, base, source, refs):
        self.n, self.half, self.units = n, n // 2, units
        self.me, self.device, self.base, self.source = me, device, base, source
        (self.s0, self.sn, self.r0, self.rn, self.bs, self.br, self.enc, self.dec,
         self.send_sem, self.recv_sem, self.bsend_sem, self.brecv_sem) = refs

    @staticmethod
    def scratch(n, blocks, units):
        half = n // 2
        first = pltpu.VMEM((units, 2, blocks, UNIT, 128), BF16)
        later = pltpu.VMEM((units, 2, half - 1, 2, blocks, UNIT, 128), BF16)
        bound = pltpu.VMEM((2, half, UNIT, 128), F32)
        return [first, later, first, later, bound, bound, bound, bound,
                pltpu.SemaphoreType.DMA((2,)), pltpu.SemaphoreType.DMA((units, 2, half)),
                pltpu.SemaphoreType.DMA, pltpu.SemaphoreType.DMA((2, half))]

    def data_copy(self, k, d, s, to):
        if s == 0:
            src, dst = self.s0.at[k, d], self.r0.at[k, d]
        else:
            src, dst = self.sn.at[k, d, s - 1], self.rn.at[k, d, s - 1]
        return pltpu.make_async_remote_copy(
            src_ref=src, dst_ref=dst, send_sem=self.send_sem.at[min(s, 1)],
            recv_sem=self.recv_sem.at[k, d, s], device_id=to, device_id_type=MESH)

    def bound_copy(self, d, s, to):
        return pltpu.make_async_remote_copy(
            src_ref=self.bs.at[d, s], dst_ref=self.br.at[d, s], send_sem=self.bsend_sem,
            recv_sem=self.brecv_sem.at[d, s], device_id=to, device_id_type=MESH)

    def neighbour(self, d):
        return self.device(lax.rem(self.me + (1 if d == 0 else self.n - 1), self.n))

    def dest(self, d, s):
        far = self.half - s
        return lax.rem(self.me + (far if d == 0 else self.n - far), self.n)

    def bounds(self, s):
        for d in (0, 1):
            to = self.neighbour(d)
            bound = self.base[self.dest(d, s)]
            if s > 0:
                self.bound_copy(d, s - 1, to).wait_recv()
                came = self.br[d, s - 1]
                self.dec[d, s - 1] = came * (1.0 / TOP)
                bound = bound + came
            self.bs[d, s] = bound
            self.enc[d, s] = TOP / bound
            self.bound_copy(d, s, to).start()

    def send(self, s, k):
        for d in (0, 1):
            to = self.neighbour(d)
            dest = self.dest(d, s)
            enc = self.enc[d, s]
            if s == 0:
                self.s0[k, d] = encode(self.source(dest, d, k), enc)
            else:
                self.data_copy(k, d, s - 1, to).wait_recv()
                dec = self.dec[d, s - 1]
                for h in (0, 1):
                    value = self.source(dest, h, k)
                    if s > 1:
                        value = value + decode(self.rn[k, d, s - 2, h], dec)
                    elif h == d:
                        value = value + decode(self.r0[k, d], dec)
                    self.sn[k, d, s - 1, h] = encode(value, enc)
            self.data_copy(k, d, s, to).start()

    def last_bounds(self, total):
        last = self.half - 1
        for d in (0, 1):
            self.bound_copy(d, last, self.neighbour(d)).wait_recv()
            self.dec[d, last] = self.br[d, last] * (1.0 / TOP)
        total[...] = self.base[self.me] + self.br[0, last] + self.br[1, last]

    def finish(self, k, store):
        last = self.half - 1
        for d in (0, 1):
            self.data_copy(k, d, last, self.neighbour(d)).wait_recv()
        for h in (0, 1):
            value = self.source(self.me, h, k)
            for d in (0, 1):
                value = value + decode(self.rn[k, d, last - 1, h], self.dec[d, last])
            store(h, value)

    def sent(self):
        to = self.neighbour(0)
        for src, dst, sem in ((self.s0, self.r0, self.send_sem.at[0]), (self.sn, self.rn, self.send_sem.at[1]),
                              (self.bs, self.br, self.bsend_sem)):
            pltpu.make_async_remote_copy(src_ref=src, dst_ref=dst, send_sem=sem, recv_sem=sem,
                                         device_id=to, device_id_type=MESH).wait_send()


class Exchange:
    def __init__(self, n, units, me, device, mid, refs):
        self.n, self.units, self.me, self.device, self.mid = n, units, me, device, mid
        self.out, self.came, self.bound, self.bcame, self.send_sem, self.recv_sem, self.bsend_sem, self.brecv_sem = refs

    @staticmethod
    def scratch(n, units):
        return [pltpu.VMEM((units, n, 2, UNIT, 128), BF16), pltpu.VMEM((units, n - 1, 2, UNIT, 128), BF16),
                pltpu.VMEM((UNIT, 128), F32), pltpu.VMEM((n - 1, UNIT, 128), F32),
                pltpu.SemaphoreType.DMA((units,)), pltpu.SemaphoreType.DMA((units,)),
                pltpu.SemaphoreType.DMA, pltpu.SemaphoreType.DMA]

    def far(self, o):
        at = lax.rem(self.me + o, self.n)
        return at, self.device(at)

    def bounds(self):
        for o in range(1, self.n):
            pltpu.make_async_remote_copy(src_ref=self.bound, dst_ref=self.bcame.at[o - 1], send_sem=self.bsend_sem,
                                         recv_sem=self.brecv_sem, device_id=self.far(o)[1], device_id_type=MESH).start()

    def send(self, k):
        enc = TOP / self.bound[...]
        for h in (0, 1):
            self.out[k, :, h] = encode(self.mid[k, h], enc)
        for o in range(1, self.n):
            at, to = self.far(o)
            pltpu.make_async_remote_copy(src_ref=self.out.at[k, at], dst_ref=self.came.at[k, o - 1],
                                         send_sem=self.send_sem.at[k], recv_sem=self.recv_sem.at[k],
                                         device_id=to, device_id_type=MESH).start()

    def all_bounds(self):
        return pltpu.make_async_remote_copy(src_ref=self.bcame, dst_ref=self.bcame, send_sem=self.bsend_sem,
                                            recv_sem=self.brecv_sem, device_id=self.far(1)[1], device_id_type=MESH)

    def all_data(self, k):
        return pltpu.make_async_remote_copy(src_ref=self.came.at[k], dst_ref=self.came.at[k], send_sem=self.send_sem.at[k],
                                            recv_sem=self.recv_sem.at[k], device_id=self.far(1)[1], device_id_type=MESH)

    def finish(self, k, store):
        self.all_data(k).wait_recv()
        for h in (0, 1):
            value = self.mid[k, h, self.me]
            for o in range(self.n - 1):
                value = value + decode(self.came[k, o, h], self.bcame[o] * (1.0 / TOP))
            store(h, value)

    def sent(self):
        self.all_bounds().wait_send()
        for k in range(self.units):
            self.all_data(k).wait_send()


class HalfExchange(Exchange):
    def __init__(self, n, units, me, device, mid, refs):
        super().__init__(n, units, me, device, mid, refs[:8])
        self.half = n // 2
        self.pre, self.got, self.near, self.total, self.pre_send, self.pre_recv, self.near_send, self.near_recv = refs[8:]
        self.others = [o for o in range(1, n) if o != self.half]

    @staticmethod
    def scratch(n, units):
        dma = pltpu.SemaphoreType.DMA
        piece = pltpu.VMEM((units, 2, UNIT, 128), BF16)
        return [pltpu.VMEM((units, n, 2, UNIT, 128), BF16), pltpu.VMEM((units, n - 2, 2, UNIT, 128), BF16),
                pltpu.VMEM((UNIT, 128), F32), pltpu.VMEM((n - 2, UNIT, 128), F32),
                dma((units,)), dma((units,)), dma, dma,
                piece, piece, pltpu.VMEM((2, UNIT, 128), F32), pltpu.VMEM((UNIT, 128), F32),
                dma, dma((units, 2)), dma, dma((2,))]

    def near_copy(self, d):
        to = self.far(1 if d == 0 else self.n - 1)[1]
        return pltpu.make_async_remote_copy(src_ref=self.bound, dst_ref=self.near.at[d], send_sem=self.near_send,
                                            recv_sem=self.near_recv.at[d], device_id=to, device_id_type=MESH)

    def pre_copy(self, k, d):
        to = self.far(1 if d == 0 else self.n - 1)[1]
        return pltpu.make_async_remote_copy(src_ref=self.pre.at[k, d], dst_ref=self.got.at[k, d], send_sem=self.pre_send,
                                            recv_sem=self.pre_recv.at[k, d], device_id=to, device_id_type=MESH)

    def near_bounds(self):
        for d in (0, 1):
            self.near_copy(d).start()

    def first(self, k):
        enc = TOP / self.bound[...]
        for d in (0, 1):
            self.pre[k, d] = encode(self.mid[k, d, self.far(self.half)[0]], enc)
            self.pre_copy(k, d).start()

    def bounds(self):
        for d in (0, 1):
            self.near_copy(d).wait_recv()
        self.total[...] = self.bound[...] + self.near[0] + self.near[1]
        for slot, o in enumerate(self.others):
            pltpu.make_async_remote_copy(src_ref=self.total, dst_ref=self.bcame.at[slot], send_sem=self.bsend_sem,
                                         recv_sem=self.brecv_sem, device_id=self.far(o)[1], device_id_type=MESH).start()

    def send(self, k):
        for d in (0, 1):
            self.pre_copy(k, d).wait_recv()
            at = self.far(self.half - 1 if d == 0 else self.half + 1)[0]
            self.mid[k, d, at] = self.mid[k, d, at] + decode(self.got[k, d], self.near[d] * (1.0 / TOP))
        enc = TOP / self.total[...]
        for h in (0, 1):
            self.out[k, :, h] = encode(self.mid[k, h], enc)
        for slot, o in enumerate(self.others):
            at, to = self.far(o)
            pltpu.make_async_remote_copy(src_ref=self.out.at[k, at], dst_ref=self.came.at[k, slot],
                                         send_sem=self.send_sem.at[k], recv_sem=self.recv_sem.at[k],
                                         device_id=to, device_id_type=MESH).start()

    def finish(self, k, store):
        self.all_data(k).wait_recv()
        for h in (0, 1):
            value = self.mid[k, h, self.me]
            for slot in range(self.n - 2):
                value = value + decode(self.came[k, slot, h], self.bcame[slot] * (1.0 / TOP))
            store(h, value)

    def sent(self):
        super().sent()
        to = self.far(1)[1]
        for src, dst, sem in ((self.pre, self.got, self.pre_send), (self.near, self.near, self.near_send)):
            pltpu.make_async_remote_copy(src_ref=src, dst_ref=dst, send_sem=sem, recv_sem=sem,
                                         device_id=to, device_id_type=MESH).wait_send()


RINGS = ((NZ, NX, KA), (NX, NZ, KB))
EXCHANGES = ((NX, KA), (NZ, KB))


def kernel(scale, tokens, up, gram, num, own, other, wown, wother, wt, upv, prod, base_z, base_x, mid_a, mid_b, fin,
           msg1, joined, recv1, msg2, recv2, gacc, own_sem, other_send, other_recv, up_sem, up_send, up_recv,
           send0, sem0, send1, sem1, send2, sem2, *refs):
    y, t = lax.axis_index("var"), lax.axis_index("tok")
    c = lax.rem(t, 2)
    chip = t // 2
    z, x = lax.rem(chip, NZ), chip // NZ
    oc = 1 - c
    sibling = (y, chip * 2 + oc)
    depth = own.shape[0]
    along_z = lambda at: (y, (x * NZ + at) * 2 + c)
    along_x = lambda at: (y, (at * NZ + z) * 2 + c)
    rows = lambda u: pl.ds(pl.multiple_of(u * UNIT, UNIT), UNIT)

    parts = (
        (8, lambda i: (2, i)),
        (3, lambda i: (lax.rem(3 + i, 4), 4)),
        (6, lambda i: (lax.rem(3 + lax.rem(i, 3), 4), 3 + 2 * (i // 3))),
        (10, lambda i: (1 + 2 * (i // 5), lax.rem(6 + lax.rem(i, 5), 8))),
        (5, lambda i: (0, lax.rem(6 + i, 8))),
    )
    starts = [sum(p[0] for p in parts[:j]) for j in range(len(parts))]

    def block_at(part, i):
        dx, dz = parts[part][1](i)
        bx, bz = lax.rem(x + dx, NX), lax.rem(z + dz, NZ)
        return bx, bz, pl.ds(pl.multiple_of((bx * NZ + bz) * 256, 256), 256)

    def own_copy(cols, at):
        return pltpu.make_async_copy(tokens.at[c, :, cols], own.at[:, cols], own_sem.at[at])

    def other_copy(cols, at):
        return pltpu.make_async_remote_copy(
            src_ref=tokens.at[oc, :, cols], dst_ref=other.at[:, cols], send_sem=other_send,
            recv_sem=other_recv.at[at], device_id=sibling, device_id_type=MESH)

    def each_block(run, which):
        for part in which:
            size = parts[part][0]
            def one(i, carry):
                run(block_at(part, i)[2], starts[part] + i)
                return carry
            lax.fori_loop(0, size, one, 0)

    front = pl.ds(0, WINDOW)
    wown_copy = pltpu.make_async_copy(tokens.at[c, :, front], wown, own_sem.at[CHIPS])
    wother_copy = pltpu.make_async_remote_copy(
        src_ref=tokens.at[oc, :, front], dst_ref=wother, send_sem=up_send.at[0], recv_sem=other_recv.at[CHIPS],
        device_id=sibling, device_id_type=MESH)
    up_own = pltpu.make_async_copy(up.at[c], upv.at[c], up_sem)
    up_other = pltpu.make_async_remote_copy(src_ref=up.at[oc], dst_ref=upv.at[c], send_sem=up_send.at[1],
                                            recv_sem=up_recv, device_id=sibling, device_id_type=MESH)

    barrier = pltpu.get_barrier_semaphore()
    peers = [sibling] + [along_z(lax.rem(z + o, NZ)) for o in (1, NZ - 1)]
    peers += [along_x(lax.rem(x + o, NX)) for o in (1, NX - 1)]
    over_y = [(lax.rem(y + o, NY), t) for o in range(1, NY)]
    for to in peers + over_y:
        pl.semaphore_signal(barrier, inc=1, device_id=to, device_id_type=MESH)
    wown_copy.start()
    pl.semaphore_wait(barrier, len(peers) + len(over_y))
    wother_copy.start()
    for which in ((0, 1), (2, 3, 4)):
        each_block(lambda cols, at: other_copy(cols, at).start(), which)
        each_block(lambda cols, at: own_copy(cols, at).start(), which)
    up_own.start()
    up_other.start()

    row = lax.broadcasted_iota(jnp.int32, (WINDOW, WINDOW), 0)
    col = lax.broadcasted_iota(jnp.int32, (WINDOW, WINDOW), 1)
    feature = ((row >> 2) & 3) * (WINDOW // NY) + (row >> 4) * 4 + (row & 3)
    pick = jnp.where(col == feature, 1.0, 0.0).astype(BF16)

    def window(ref):
        return lax.dot_general(pick, ref[...], (((1,), (1,)), ((), ())), preferred_element_type=F32).astype(BF16)

    wown_copy.wait()
    wt[:, :depth] = window(wown)
    for ref in (base_z, base_x):
        ref[...] = jnp.full(ref.shape, 1e-33, F32)

    wother_copy.wait_recv()
    wt[:, depth:] = window(wother)

    def multiply(part):
        def one(i, carry):
            bx, bz, cols = block_at(part, i)
            at = starts[part] + i
            own_copy(cols, at).wait()
            other_copy(cols, at).wait_recv()
            product = jnp.dot(wt[:, :depth], own[:, cols], preferred_element_type=F32)
            product = product + jnp.dot(wt[:, depth:], other[:, cols], preferred_element_type=F32)
            prod[bx, bz, 0] = product[:, :128]
            prod[bx, bz, 1] = product[:, 128:]
            top = jnp.max(jnp.abs(product).reshape(UNITS, UNIT, 256), axis=0)
            top = jnp.maximum(top[:, :128], top[:, 128:])
            base_z[bz] = jnp.maximum(base_z[bz], top)
            base_x[bx] = jnp.maximum(base_x[bx], top)
            return carry
        lax.fori_loop(0, parts[part][0], one, 0)

    sizes = (12, 12, 8, 16)
    split = [refs[sum(sizes[:j]):sum(sizes[:j + 1])] for j in range(4)]
    az = Ring(*RINGS[0], z, along_z, base_z, lambda dest, h, k: prod[:, dest, h, rows(k), :], split[0])
    bx = Ring(*RINGS[1], x, along_x, base_x, lambda dest, h, k: prod[dest, :, h, rows(KA + k), :], split[1])
    ax = Exchange(*EXCHANGES[0], x, along_x, mid_a, split[2])
    bz = HalfExchange(*EXCHANGES[1], z, along_z, mid_b, split[3])

    def numerators(j):
        total = None
        for h in (0, 1):
            g = jnp.concatenate([fin[2 * j, h], fin[2 * j + 1, h]], axis=0)
            high = g.astype(BF16)
            low = (g - high.astype(F32)).astype(BF16)
            term = jnp.dot(jnp.concatenate([high, low], axis=0), upv[h], preferred_element_type=F32)
            total = term if total is None else total + term
        total = total[:2 * UNIT] + total[2 * UNIT:]
        tiles = total.reshape(2 * UNIT, 8, 128)
        for p in range(NY):
            for half in (0, 1):
                for ab in (0, 1):
                    for i in (0, 1):
                        msg1[j, half, p, 2 * ab + i] = tiles[UNIT * ab + 4 * p + 2 * i + half]
                    msg1[j, half, p, 4, 4 * ab:4 * ab + 4, :] = fin[2 * j + ab, half, 4 * p:4 * p + 4, :]
        core_copy(j).start()

    def core_copy(j):
        return pltpu.make_async_remote_copy(src_ref=msg1.at[j, oc], dst_ref=joined.at[j], send_sem=send0.at[j],
                                            recv_sem=sem0.at[j], device_id=sibling, device_id_type=MESH)

    def join(j):
        core_copy(j).wait_recv()
        for p in range(NY):
            msg1[j, c, p] = msg1[j, c, p] + joined[j, p]
        for o in range(1, NY):
            p = lax.rem(y + o, NY)
            pltpu.make_async_remote_copy(src_ref=msg1.at[j, c, p], dst_ref=recv1.at[j, o - 1], send_sem=send1.at[j],
                                         recv_sem=sem1.at[j], device_id=(p, t), device_id_type=MESH).start()

    def pair_copies(j):
        return pltpu.make_async_remote_copy(src_ref=recv1.at[j], dst_ref=recv1.at[j], send_sem=send1.at[j],
                                            recv_sem=sem1.at[j], device_id=sibling, device_id_type=MESH)

    def row_copy(src, to_chip):
        slot = lax.rem(to_chip - chip + CHIPS, CHIPS) - 1
        return pltpu.make_async_remote_copy(src_ref=src, dst_ref=recv2.at[slot], send_sem=send2, recv_sem=sem2,
                                            device_id=(y, to_chip * 2 + c), device_id_type=MESH)

    def pass_on(j):
        pair_copies(j).wait_recv()
        total = msg1[j, c, y]
        for o in range(NY - 1):
            total = total + recv1[j, o]
        msg2[j] = total[:4]
        gacc[j] = total[4]

        def row_out(i, carry):
            u = 2 * j + i // 2
            to = (u // 4) * NZ + 2 * lax.rem(u, 4) + lax.rem(i, 2)

            @pl.when(to == chip)
            def _():
                recv2[CHIPS - 1] = msg2[j, i]

            @pl.when(to != chip)
            def _():
                row_copy(msg2.at[j, i], to).start()
            return carry

        lax.fori_loop(0, 4, row_out, 0)

    def run(step, low, high):
        def one(k, carry):
            step(k)
            return carry
        lax.fori_loop(low, high, one, 0)

    def put(ref, k):
        def store(h, value):
            ref[k, h] = value
        return store

    def put_final(u):
        def store(h, value):
            fin[u, h] = value * scale
        return store

    def a_turn(k):
        az.finish(k, put(mid_a, k))
        ax.send(k)

    def b_turn(k):
        bx.finish(k, put(mid_b, k))
        bz.first(k)

    def a_pair(j):
        for i in (0, 1):
            ax.finish(2 * j + i, put_final(2 * j + i))
        numerators(j)

    def b_pair(j):
        for i in (0, 1):
            bz.finish(2 * j + i, put_final(KA + 2 * j + i))
        numerators(KA // 2 + j)

    def at_tick(at, start, count, step, prepare=None):
        def now():
            if prepare is not None:
                pl.when(at == start)(prepare)
            step(at - start)
        pl.when(jnp.logical_and(at >= start, at < start + count))(now)

    def two(step):
        return lambda m: run(step, 2 * m, 2 * m + 2)

    def every_other(step):
        return lambda m: pl.when(lax.rem(m, 2) == 0)(lambda: step(m // 2))

    a_send = lambda s: functools.partial(az.send, s)
    b_send = lambda s: functools.partial(bx.send, s)
    half_a, half_b = KA // 2, KB // 2

    def a_meet():
        az.last_bounds(ax.bound)
        ax.bounds()

    def b_meet():
        bx.last_bounds(bz.bound)
        bz.near_bounds()

    multiply(0)
    bx.bounds(0)
    run(b_send(0), 0, KB)
    multiply(1)
    az.bounds(0)
    run(a_send(0), 0, KA)
    multiply(2)
    az.bounds(1)
    run(a_send(1), 0, KA)
    multiply(3)
    bx.bounds(1)
    b_send(1)(0)
    multiply(4)
    up_own.wait()
    up_other.wait_recv()

    def tick(at, carry):
        at_tick(at, A2, half_a, two(a_send(2)), lambda: az.bounds(2))
        at_tick(at, A3, half_a, two(a_send(3)), lambda: az.bounds(3))
        at_tick(at, 1, KB - 1, lambda k: bx.send(1, k + 1))
        at_tick(at, AT, half_a, two(a_turn), a_meet)
        at_tick(at, BT, KB, b_turn, b_meet)
        at_tick(at, BE, KB, bz.send, bz.bounds)
        at_tick(at, AP, half_a, a_pair, lambda: ax.all_bounds().wait_recv())
        at_tick(at, BP, KB - 1, every_other(b_pair), lambda: bz.all_bounds().wait_recv())
        at_tick(at, AP + 1, half_a, join)
        at_tick(at, BP + 1, KB - 1, every_other(lambda j: join(half_a + j)))
        at_tick(at, AP + 4, half_a, pass_on)
        at_tick(at, BP + 5, KB - 1, every_other(lambda j: pass_on(half_a + j)))
        return carry

    lax.fori_loop(0, BP + KB, tick, 0)
    run(pass_on, PAIRS - 2, PAIRS)

    for j in range(PAIRS):
        gram[8 * j:8 * j + 8, :] = gacc[j]
    all_rows = pltpu.make_async_remote_copy(src_ref=recv2.at[pl.ds(0, CHIPS - 1)], dst_ref=recv2.at[pl.ds(0, CHIPS - 1)],
                                            send_sem=send2, recv_sem=sem2, device_id=sibling, device_id_type=MESH)
    all_rows.wait_send()
    for j in range(PAIRS):
        pair_copies(j).wait_send()
        core_copy(j).wait_send()
    for group in (az, bx, ax, bz):
        group.sent()
    wother_copy.wait_send()
    up_other.wait_send()
    pltpu.make_async_remote_copy(src_ref=tokens.at[oc], dst_ref=other, send_sem=other_send, recv_sem=other_send,
                                 device_id=sibling, device_id_type=MESH).wait_send()
    all_rows.wait_recv()
    num[...] = jnp.sum(recv2[...], axis=0)


def write(gram, num, gram_out, num_out):
    gram_out[...] = gram[...]
    for i in range(8):
        num_out[0:1, 128 * i:128 * (i + 1)] = num[i:i + 1, :]


def body(tokens, up_panel):
    variants, depth, width = tokens.shape
    block, panel = up_panel.shape[1:]
    scale = 1.0 / (depth * lax.axis_size("tok"))
    dma = pltpu.SemaphoreType.DMA
    scratch = [
        pltpu.VMEM((depth, width), BF16),
        pltpu.VMEM((depth, width), BF16),
        pltpu.VMEM((depth, WINDOW), BF16),
        pltpu.VMEM((depth, WINDOW), BF16),
        pltpu.VMEM((WINDOW, 2 * depth), BF16),
        pltpu.VMEM((2, block, panel), BF16),
        pltpu.VMEM((NX, NZ, 2, WINDOW, 128), F32),
        pltpu.VMEM((NZ, UNIT, 128), F32),
        pltpu.VMEM((NX, UNIT, 128), F32),
        pltpu.VMEM((KA, 2, NX, UNIT, 128), F32),
        pltpu.VMEM((KB, 2, NZ, UNIT, 128), F32),
        pltpu.VMEM((UNITS, 2, UNIT, 128), F32),
        pltpu.VMEM((PAIRS, 2, NY, 5, 8, 128), F32),
        pltpu.VMEM((PAIRS, NY, 5, 8, 128), F32),
        pltpu.VMEM((PAIRS, NY - 1, 5, 8, 128), F32),
        pltpu.VMEM((PAIRS, 4, 8, 128), F32),
        pltpu.VMEM((CHIPS, 8, 128), F32),
        pltpu.VMEM((PAIRS, 8, 128), F32),
        dma((CHIPS + 1,)), dma, dma((CHIPS + 1,)), dma, dma((2,)), dma,
        dma((PAIRS,)), dma((PAIRS,)), dma((PAIRS,)), dma((PAIRS,)), dma, dma,
    ]
    for shape in RINGS:
        scratch += Ring.scratch(*shape)
    scratch += Exchange.scratch(*EXCHANGES[0]) + HalfExchange.scratch(*EXCHANGES[1])
    gram, num = pl.pallas_call(
        functools.partial(kernel, scale),
        out_shape=(
            jax.ShapeDtypeStruct((WINDOW // NY, block), F32),
            jax.ShapeDtypeStruct((8, panel // 8), F32),
        ),
        in_specs=[pl.BlockSpec(memory_space=pl.ANY)] * 2,
        out_specs=(pl.BlockSpec(memory_space=pltpu.VMEM),) * 2,
        scratch_shapes=scratch,
        compiler_params=pltpu.CompilerParams(
            collective_id=0, has_side_effects=True, vmem_limit_bytes=60 * 2**20
        ),
    )(tokens, up_panel)
    return pl.pallas_call(
        write,
        out_shape=(
            jax.ShapeDtypeStruct((WINDOW // NY, block), F32),
            jax.ShapeDtypeStruct((1, panel), F32),
        ),
    )(gram, num)


def solution(mesh):
    return jax.shard_map(
        body,
        mesh=mesh,
        in_specs=(P("var", "tok", None), P("var", "tok", None)),
        out_specs=(P("var", "tok"), P(("var", "tok"), None)),
        check_vma=False,
    )
```

```python
import functools

import jax
import jax.numpy as jnp
from jax import lax
from jax.experimental import pallas as pl
from jax.experimental.pallas import tpu as pltpu
from jax.sharding import PartitionSpec as P

WINDOW = 256
NX, NZ, NY = 4, 8, 4
CHIPS = NX * NZ
UNIT = 16
UNITS = WINDOW // UNIT
KA = 6
KB = UNITS - KA
PAIRS = UNITS // 2
A2, A3, AT, BT, BE, AP, BP = 1, 4, 10, 3, 6, 14, 11
POWER = 9
TOP = 2.0**13.8
MESH = pl.DeviceIdType.MESH
F32, BF16 = jnp.float32, jnp.bfloat16


def encode(value, factor):
    t = value * factor
    t2 = t * t
    t4 = t2 * t2
    return (t4 * t4 * t).astype(BF16)


def decode(code, factor):
    y = code.astype(F32)
    root = jnp.exp2(jnp.log(jnp.maximum(jnp.abs(y), 1e-38)) * (1.4426950408889634 / POWER))
    return jnp.where(y < 0, -root, root) * factor


class Ring:
    def __init__(self, n, blocks, units, me, device, base, source, refs):
        self.n, self.half, self.units = n, n // 2, units
        self.me, self.device, self.base, self.source = me, device, base, source
        (self.s0, self.sn, self.r0, self.rn, self.bs, self.br, self.enc, self.dec,
         self.send_sem, self.recv_sem, self.bsend_sem, self.brecv_sem) = refs

    @staticmethod
    def scratch(n, blocks, units):
        half = n // 2
        first = pltpu.VMEM((units, 2, blocks, UNIT, 128), BF16)
        later = pltpu.VMEM((units, 2, half - 1, 2, blocks, UNIT, 128), BF16)
        bound = pltpu.VMEM((2, half, UNIT, 128), F32)
        return [first, later, first, later, bound, bound, bound, bound,
                pltpu.SemaphoreType.DMA((2,)), pltpu.SemaphoreType.DMA((units, 2, half)),
                pltpu.SemaphoreType.DMA, pltpu.SemaphoreType.DMA((2, half))]

    def data_copy(self, k, d, s, to):
        if s == 0:
            src, dst = self.s0.at[k, d], self.r0.at[k, d]
        else:
            src, dst = self.sn.at[k, d, s - 1], self.rn.at[k, d, s - 1]
        return pltpu.make_async_remote_copy(
            src_ref=src, dst_ref=dst, send_sem=self.send_sem.at[min(s, 1)],
            recv_sem=self.recv_sem.at[k, d, s], device_id=to, device_id_type=MESH)

    def bound_copy(self, d, s, to):
        return pltpu.make_async_remote_copy(
            src_ref=self.bs.at[d, s], dst_ref=self.br.at[d, s], send_sem=self.bsend_sem,
            recv_sem=self.brecv_sem.at[d, s], device_id=to, device_id_type=MESH)

    def neighbour(self, d):
        return self.device(lax.rem(self.me + (1 if d == 0 else self.n - 1), self.n))

    def dest(self, d, s):
        far = self.half - s
        return lax.rem(self.me + (far if d == 0 else self.n - far), self.n)

    def bounds(self, s):
        for d in (0, 1):
            to = self.neighbour(d)
            bound = self.base[self.dest(d, s)]
            if s > 0:
                self.bound_copy(d, s - 1, to).wait_recv()
                came = self.br[d, s - 1]
                self.dec[d, s - 1] = came * (1.0 / TOP)
                bound = bound + came
            self.bs[d, s] = bound
            self.enc[d, s] = TOP / bound
            self.bound_copy(d, s, to).start()

    def send(self, s, k):
        for d in (0, 1):
            to = self.neighbour(d)
            dest = self.dest(d, s)
            enc = self.enc[d, s]
            if s == 0:
                self.s0[k, d] = encode(self.source(dest, d, k), enc)
            else:
                self.data_copy(k, d, s - 1, to).wait_recv()
                dec = self.dec[d, s - 1]
                for h in (0, 1):
                    value = self.source(dest, h, k)
                    if s > 1:
                        value = value + decode(self.rn[k, d, s - 2, h], dec)
                    elif h == d:
                        value = value + decode(self.r0[k, d], dec)
                    self.sn[k, d, s - 1, h] = encode(value, enc)
            self.data_copy(k, d, s, to).start()

    def last_bounds(self, total):
        last = self.half - 1
        for d in (0, 1):
            self.bound_copy(d, last, self.neighbour(d)).wait_recv()
            self.dec[d, last] = self.br[d, last] * (1.0 / TOP)
        total[...] = self.base[self.me] + self.br[0, last] + self.br[1, last]

    def finish(self, k, store):
        last = self.half - 1
        for d in (0, 1):
            self.data_copy(k, d, last, self.neighbour(d)).wait_recv()
        for h in (0, 1):
            value = self.source(self.me, h, k)
            for d in (0, 1):
                value = value + decode(self.rn[k, d, last - 1, h], self.dec[d, last])
            store(h, value)

    def sent(self):
        to = self.neighbour(0)
        for src, dst, sem in ((self.s0, self.r0, self.send_sem.at[0]), (self.sn, self.rn, self.send_sem.at[1]),
                              (self.bs, self.br, self.bsend_sem)):
            pltpu.make_async_remote_copy(src_ref=src, dst_ref=dst, send_sem=sem, recv_sem=sem,
                                         device_id=to, device_id_type=MESH).wait_send()


class Exchange:
    def __init__(self, n, units, me, device, mid, refs):
        self.n, self.units, self.me, self.device, self.mid = n, units, me, device, mid
        self.out, self.came, self.bound, self.bcame, self.send_sem, self.recv_sem, self.bsend_sem, self.brecv_sem = refs

    @staticmethod
    def scratch(n, units):
        return [pltpu.VMEM((units, n, 2, UNIT, 128), BF16), pltpu.VMEM((units, n - 1, 2, UNIT, 128), BF16),
                pltpu.VMEM((UNIT, 128), F32), pltpu.VMEM((n - 1, UNIT, 128), F32),
                pltpu.SemaphoreType.DMA((units,)), pltpu.SemaphoreType.DMA((units,)),
                pltpu.SemaphoreType.DMA, pltpu.SemaphoreType.DMA]

    def far(self, o):
        at = lax.rem(self.me + o, self.n)
        return at, self.device(at)

    def bounds(self):
        for o in range(1, self.n):
            pltpu.make_async_remote_copy(src_ref=self.bound, dst_ref=self.bcame.at[o - 1], send_sem=self.bsend_sem,
                                         recv_sem=self.brecv_sem, device_id=self.far(o)[1], device_id_type=MESH).start()

    def send(self, k):
        enc = TOP / self.bound[...]
        for h in (0, 1):
            self.out[k, :, h] = encode(self.mid[k, h], enc)
        for o in sorted(range(1, self.n), key=lambda o: abs(o - self.n // 2)):
            at, to = self.far(o)
            pltpu.make_async_remote_copy(src_ref=self.out.at[k, at], dst_ref=self.came.at[k, o - 1],
                                         send_sem=self.send_sem.at[k], recv_sem=self.recv_sem.at[k],
                                         device_id=to, device_id_type=MESH).start()

    def all_bounds(self):
        return pltpu.make_async_remote_copy(src_ref=self.bcame, dst_ref=self.bcame, send_sem=self.bsend_sem,
                                            recv_sem=self.brecv_sem, device_id=self.far(1)[1], device_id_type=MESH)

    def all_data(self, k):
        return pltpu.make_async_remote_copy(src_ref=self.came.at[k], dst_ref=self.came.at[k], send_sem=self.send_sem.at[k],
                                            recv_sem=self.recv_sem.at[k], device_id=self.far(1)[1], device_id_type=MESH)

    def finish(self, k, store):
        self.all_data(k).wait_recv()
        for h in (0, 1):
            value = self.mid[k, h, self.me]
            for o in range(self.n - 1):
                value = value + decode(self.came[k, o, h], self.bcame[o] * (1.0 / TOP))
            store(h, value)

    def sent(self):
        self.all_bounds().wait_send()
        for k in range(self.units):
            self.all_data(k).wait_send()


class HalfExchange(Exchange):
    def __init__(self, n, units, me, device, mid, refs):
        super().__init__(n, units, me, device, mid, refs[:8])
        self.half = n // 2
        self.pre, self.got, self.near, self.total, self.pre_send, self.pre_recv, self.near_send, self.near_recv = refs[8:]
        self.others = sorted((o for o in range(1, n) if o != self.half), key=lambda o: abs(o - self.half))

    @staticmethod
    def scratch(n, units):
        dma = pltpu.SemaphoreType.DMA
        piece = pltpu.VMEM((units, 2, UNIT, 128), BF16)
        return [pltpu.VMEM((units, n, 2, UNIT, 128), BF16), pltpu.VMEM((units, n - 2, 2, UNIT, 128), BF16),
                pltpu.VMEM((UNIT, 128), F32), pltpu.VMEM((n - 2, UNIT, 128), F32),
                dma((units,)), dma((units,)), dma, dma,
                piece, piece, pltpu.VMEM((2, UNIT, 128), F32), pltpu.VMEM((UNIT, 128), F32),
                dma, dma((units, 2)), dma, dma((2,))]

    def near_copy(self, d):
        to = self.far(1 if d == 0 else self.n - 1)[1]
        return pltpu.make_async_remote_copy(src_ref=self.bound, dst_ref=self.near.at[d], send_sem=self.near_send,
                                            recv_sem=self.near_recv.at[d], device_id=to, device_id_type=MESH)

    def pre_copy(self, k, d):
        to = self.far(1 if d == 0 else self.n - 1)[1]
        return pltpu.make_async_remote_copy(src_ref=self.pre.at[k, d], dst_ref=self.got.at[k, d], send_sem=self.pre_send,
                                            recv_sem=self.pre_recv.at[k, d], device_id=to, device_id_type=MESH)

    def near_bounds(self):
        for d in (0, 1):
            self.near_copy(d).start()

    def first(self, k):
        enc = TOP / self.bound[...]
        for d in (0, 1):
            self.pre[k, d] = encode(self.mid[k, d, self.far(self.half)[0]], enc)
            self.pre_copy(k, d).start()

    def bounds(self):
        for d in (0, 1):
            self.near_copy(d).wait_recv()
        self.total[...] = self.bound[...] + self.near[0] + self.near[1]
        for slot, o in enumerate(self.others):
            pltpu.make_async_remote_copy(src_ref=self.total, dst_ref=self.bcame.at[slot], send_sem=self.bsend_sem,
                                         recv_sem=self.brecv_sem, device_id=self.far(o)[1], device_id_type=MESH).start()

    def send(self, k):
        for d in (0, 1):
            self.pre_copy(k, d).wait_recv()
            at = self.far(self.half - 1 if d == 0 else self.half + 1)[0]
            self.mid[k, d, at] = self.mid[k, d, at] + decode(self.got[k, d], self.near[d] * (1.0 / TOP))
        enc = TOP / self.total[...]
        for h in (0, 1):
            self.out[k, :, h] = encode(self.mid[k, h], enc)
        for slot, o in enumerate(self.others):
            at, to = self.far(o)
            pltpu.make_async_remote_copy(src_ref=self.out.at[k, at], dst_ref=self.came.at[k, slot],
                                         send_sem=self.send_sem.at[k], recv_sem=self.recv_sem.at[k],
                                         device_id=to, device_id_type=MESH).start()

    def finish(self, k, store):
        self.all_data(k).wait_recv()
        for h in (0, 1):
            value = self.mid[k, h, self.me]
            for slot in range(self.n - 2):
                value = value + decode(self.came[k, slot, h], self.bcame[slot] * (1.0 / TOP))
            store(h, value)

    def sent(self):
        super().sent()
        to = self.far(1)[1]
        for src, dst, sem in ((self.pre, self.got, self.pre_send), (self.near, self.near, self.near_send)):
            pltpu.make_async_remote_copy(src_ref=src, dst_ref=dst, send_sem=sem, recv_sem=sem,
                                         device_id=to, device_id_type=MESH).wait_send()


RINGS = ((NZ, NX, KA), (NX, NZ, KB))
EXCHANGES = ((NX, KA), (NZ, KB))


def kernel(scale, tokens, up, gram, num, own, other, wown, wother, wt, upv, prod, base_z, base_x, mid_a, mid_b, fin,
           msg1, joined, recv1, msg2, recv2, gacc, own_sem, other_send, other_recv, up_sem, up_send, up_recv,
           send0, sem0, send1, sem1, send2, sem2, *refs):
    y, t = lax.axis_index("var"), lax.axis_index("tok")
    c = lax.rem(t, 2)
    chip = t // 2
    z, x = lax.rem(chip, NZ), chip // NZ
    oc = 1 - c
    sibling = (y, chip * 2 + oc)
    depth = own.shape[0]
    along_z = lambda at: (y, (x * NZ + at) * 2 + c)
    along_x = lambda at: (y, (at * NZ + z) * 2 + c)
    rows = lambda u: pl.ds(pl.multiple_of(u * UNIT, UNIT), UNIT)

    parts = (
        (8, lambda i: (2, i)),
        (3, lambda i: (lax.rem(3 + i, 4), 4)),
        (6, lambda i: (lax.rem(3 + lax.rem(i, 3), 4), 3 + 2 * (i // 3))),
        (10, lambda i: (1 + 2 * (i // 5), lax.rem(6 + lax.rem(i, 5), 8))),
        (5, lambda i: (0, lax.rem(6 + i, 8))),
    )
    starts = [sum(p[0] for p in parts[:j]) for j in range(len(parts))]

    def block_at(part, i):
        dx, dz = parts[part][1](i)
        bx, bz = lax.rem(x + dx, NX), lax.rem(z + dz, NZ)
        return bx, bz, pl.ds(pl.multiple_of((bx * NZ + bz) * 256, 256), 256)

    def own_copy(cols, at):
        return pltpu.make_async_copy(tokens.at[c, :, cols], own.at[:, cols], own_sem.at[at])

    def other_copy(cols, at):
        return pltpu.make_async_remote_copy(
            src_ref=tokens.at[oc, :, cols], dst_ref=other.at[:, cols], send_sem=other_send,
            recv_sem=other_recv.at[at], device_id=sibling, device_id_type=MESH)

    def each_block(run, which):
        for part in which:
            size = parts[part][0]
            def one(i, carry):
                run(block_at(part, i)[2], starts[part] + i)
                return carry
            lax.fori_loop(0, size, one, 0)

    front = pl.ds(0, WINDOW)
    wown_copy = pltpu.make_async_copy(tokens.at[c, :, front], wown, own_sem.at[CHIPS])
    wother_copy = pltpu.make_async_remote_copy(
        src_ref=tokens.at[oc, :, front], dst_ref=wother, send_sem=up_send.at[0], recv_sem=other_recv.at[CHIPS],
        device_id=sibling, device_id_type=MESH)
    up_own = pltpu.make_async_copy(up.at[c], upv.at[c], up_sem)
    up_other = pltpu.make_async_remote_copy(src_ref=up.at[oc], dst_ref=upv.at[c], send_sem=up_send.at[1],
                                            recv_sem=up_recv, device_id=sibling, device_id_type=MESH)

    barrier = pltpu.get_barrier_semaphore()
    peers = [sibling] + [along_z(lax.rem(z + o, NZ)) for o in (1, NZ - 1)]
    peers += [along_x(lax.rem(x + o, NX)) for o in (1, NX - 1)]
    over_y = [(lax.rem(y + o, NY), t) for o in range(1, NY)]
    for to in peers + over_y:
        pl.semaphore_signal(barrier, inc=1, device_id=to, device_id_type=MESH)
    wown_copy.start()
    pl.semaphore_wait(barrier, len(peers) + len(over_y))
    wother_copy.start()
    for which in ((0, 1), (2, 3, 4)):
        each_block(lambda cols, at: other_copy(cols, at).start(), which)
        each_block(lambda cols, at: own_copy(cols, at).start(), which)
    up_own.start()
    up_other.start()

    row = lax.broadcasted_iota(jnp.int32, (WINDOW, WINDOW), 0)
    col = lax.broadcasted_iota(jnp.int32, (WINDOW, WINDOW), 1)
    feature = ((row >> 2) & 3) * (WINDOW // NY) + (row >> 4) * 4 + (row & 3)
    pick = jnp.where(col == feature, 1.0, 0.0).astype(BF16)

    def window(ref):
        return lax.dot_general(pick, ref[...], (((1,), (1,)), ((), ())), preferred_element_type=F32).astype(BF16)

    wown_copy.wait()
    wt[:, :depth] = window(wown)
    for ref in (base_z, base_x):
        ref[...] = jnp.full(ref.shape, 1e-33, F32)

    wother_copy.wait_recv()
    wt[:, depth:] = window(wother)

    def multiply(part):
        def one(i, carry):
            bx, bz, cols = block_at(part, i)
            at = starts[part] + i
            own_copy(cols, at).wait()
            other_copy(cols, at).wait_recv()
            product = jnp.dot(wt[:, :depth], own[:, cols], preferred_element_type=F32)
            product = product + jnp.dot(wt[:, depth:], other[:, cols], preferred_element_type=F32)
            prod[bx, bz, 0] = product[:, :128]
            prod[bx, bz, 1] = product[:, 128:]
            top = jnp.max(jnp.abs(product).reshape(UNITS, UNIT, 256), axis=0)
            top = jnp.maximum(top[:, :128], top[:, 128:])
            base_z[bz] = jnp.maximum(base_z[bz], top)
            base_x[bx] = jnp.maximum(base_x[bx], top)
            return carry
        lax.fori_loop(0, parts[part][0], one, 0)

    sizes = (12, 12, 8, 16)
    split = [refs[sum(sizes[:j]):sum(sizes[:j + 1])] for j in range(4)]
    az = Ring(*RINGS[0], z, along_z, base_z, lambda dest, h, k: prod[:, dest, h, rows(k), :], split[0])
    bx = Ring(*RINGS[1], x, along_x, base_x, lambda dest, h, k: prod[dest, :, h, rows(KA + k), :], split[1])
    ax = Exchange(*EXCHANGES[0], x, along_x, mid_a, split[2])
    bz = HalfExchange(*EXCHANGES[1], z, along_z, mid_b, split[3])

    def numerators(j):
        total = None
        for h in (0, 1):
            g = jnp.concatenate([fin[2 * j, h], fin[2 * j + 1, h]], axis=0)
            high = g.astype(BF16)
            low = (g - high.astype(F32)).astype(BF16)
            term = jnp.dot(jnp.concatenate([high, low], axis=0), upv[h], preferred_element_type=F32)
            total = term if total is None else total + term
        total = total[:2 * UNIT] + total[2 * UNIT:]
        tiles = total.reshape(2 * UNIT, 8, 128)
        for p in range(NY):
            for half in (0, 1):
                for ab in (0, 1):
                    for i in (0, 1):
                        msg1[j, half, p, 2 * ab + i] = tiles[UNIT * ab + 4 * p + 2 * i + half]
                    msg1[j, half, p, 4, 4 * ab:4 * ab + 4, :] = fin[2 * j + ab, half, 4 * p:4 * p + 4, :]
        core_copy(j).start()

    def core_copy(j):
        return pltpu.make_async_remote_copy(src_ref=msg1.at[j, oc], dst_ref=joined.at[j], send_sem=send0.at[j],
                                            recv_sem=sem0.at[j], device_id=sibling, device_id_type=MESH)

    def join(j):
        core_copy(j).wait_recv()
        for o in (2, 1, 3, 0):
            p = lax.rem(y + o, NY)
            msg1[j, c, p] = msg1[j, c, p] + joined[j, p]
            if o == 0:
                break
            pltpu.make_async_remote_copy(src_ref=msg1.at[j, c, p], dst_ref=recv1.at[j, o - 1], send_sem=send1.at[j],
                                         recv_sem=sem1.at[j], device_id=(p, t), device_id_type=MESH).start()

    def pair_copies(j):
        return pltpu.make_async_remote_copy(src_ref=recv1.at[j], dst_ref=recv1.at[j], send_sem=send1.at[j],
                                            recv_sem=sem1.at[j], device_id=sibling, device_id_type=MESH)

    def row_copy(src, to_chip):
        slot = lax.rem(to_chip - chip + CHIPS, CHIPS) - 1
        return pltpu.make_async_remote_copy(src_ref=src, dst_ref=recv2.at[slot], send_sem=send2, recv_sem=sem2,
                                            device_id=(y, to_chip * 2 + c), device_id_type=MESH)

    def pass_on(j):
        pair_copies(j).wait_recv()
        total = msg1[j, c, y]
        for o in range(NY - 1):
            total = total + recv1[j, o]
        msg2[j] = total[:4]
        gacc[j] = total[4]

        def row_out(i, carry):
            u = 2 * j + i // 2
            to = (u // 4) * NZ + 2 * lax.rem(u, 4) + lax.rem(i, 2)

            @pl.when(to == chip)
            def _():
                recv2[CHIPS - 1] = msg2[j, i]

            @pl.when(to != chip)
            def _():
                row_copy(msg2.at[j, i], to).start()
            return carry

        lax.fori_loop(0, 4, row_out, 0)

    def run(step, low, high):
        def one(k, carry):
            step(k)
            return carry
        lax.fori_loop(low, high, one, 0)

    def put(ref, k):
        def store(h, value):
            ref[k, h] = value
        return store

    def put_final(u):
        def store(h, value):
            fin[u, h] = value * scale
        return store

    def a_turn(k):
        az.finish(k, put(mid_a, k))
        ax.send(k)

    def b_turn(k):
        bx.finish(k, put(mid_b, k))
        bz.first(k)

    def a_pair(j):
        for i in (0, 1):
            ax.finish(2 * j + i, put_final(2 * j + i))
        numerators(j)

    def b_pair(j):
        for i in (0, 1):
            bz.finish(2 * j + i, put_final(KA + 2 * j + i))
        numerators(KA // 2 + j)

    def at_tick(at, start, count, step, prepare=None):
        def now():
            if prepare is not None:
                pl.when(at == start)(prepare)
            step(at - start)
        pl.when(jnp.logical_and(at >= start, at < start + count))(now)

    def two(step):
        return lambda m: run(step, 2 * m, 2 * m + 2)

    def every_other(step):
        return lambda m: pl.when(lax.rem(m, 2) == 0)(lambda: step(m // 2))

    a_send = lambda s: functools.partial(az.send, s)
    b_send = lambda s: functools.partial(bx.send, s)
    half_a, half_b = KA // 2, KB // 2

    def a_meet():
        az.last_bounds(ax.bound)
        ax.bounds()

    def b_meet():
        bx.last_bounds(bz.bound)
        bz.near_bounds()

    multiply(0)
    bx.bounds(0)
    run(b_send(0), 0, KB)
    multiply(1)
    az.bounds(0)
    run(a_send(0), 0, KA)
    multiply(2)
    az.bounds(1)
    run(a_send(1), 0, KA)
    multiply(3)
    bx.bounds(1)
    b_send(1)(0)
    multiply(4)
    up_own.wait()
    up_other.wait_recv()

    def tick(at, carry):
        at_tick(at, A2, half_a, two(a_send(2)), lambda: az.bounds(2))
        at_tick(at, A3, half_a, two(a_send(3)), lambda: az.bounds(3))
        at_tick(at, 1, KB - 1, lambda k: bx.send(1, k + 1))
        at_tick(at, AT, half_a, two(a_turn), a_meet)
        at_tick(at, BT, KB, b_turn, b_meet)
        at_tick(at, BE, KB, bz.send, bz.bounds)
        at_tick(at, AP, half_a, a_pair, lambda: ax.all_bounds().wait_recv())
        at_tick(at, BP, KB - 1, every_other(b_pair), lambda: bz.all_bounds().wait_recv())
        at_tick(at, AP + 1, half_a, join)
        at_tick(at, BP + 1, KB - 1, every_other(lambda j: join(half_a + j)))
        at_tick(at, AP + 4, half_a, pass_on)
        at_tick(at, BP + 5, KB - 1, every_other(lambda j: pass_on(half_a + j)))
        return carry

    lax.fori_loop(0, BP + KB, tick, 0)
    run(pass_on, PAIRS - 2, PAIRS)

    for j in range(PAIRS):
        gram[8 * j:8 * j + 8, :] = gacc[j]
    all_rows = pltpu.make_async_remote_copy(src_ref=recv2.at[pl.ds(0, CHIPS - 1)], dst_ref=recv2.at[pl.ds(0, CHIPS - 1)],
                                            send_sem=send2, recv_sem=sem2, device_id=sibling, device_id_type=MESH)
    all_rows.wait_send()
    for j in range(PAIRS):
        pair_copies(j).wait_send()
        core_copy(j).wait_send()
    for group in (az, bx, ax, bz):
        group.sent()
    wother_copy.wait_send()
    up_other.wait_send()
    pltpu.make_async_remote_copy(src_ref=tokens.at[oc], dst_ref=other, send_sem=other_send, recv_sem=other_send,
                                 device_id=sibling, device_id_type=MESH).wait_send()
    all_rows.wait_recv()
    num[...] = jnp.sum(recv2[...], axis=0)


def write(gram, num, gram_out, num_out):
    gram_out[...] = gram[...]
    for i in range(8):
        num_out[0:1, 128 * i:128 * (i + 1)] = num[i:i + 1, :]


def body(tokens, up_panel):
    variants, depth, width = tokens.shape
    block, panel = up_panel.shape[1:]
    scale = 1.0 / (depth * lax.axis_size("tok"))
    dma = pltpu.SemaphoreType.DMA
    scratch = [
        pltpu.VMEM((depth, width), BF16),
        pltpu.VMEM((depth, width), BF16),
        pltpu.VMEM((depth, WINDOW), BF16),
        pltpu.VMEM((depth, WINDOW), BF16),
        pltpu.VMEM((WINDOW, 2 * depth), BF16),
        pltpu.VMEM((2, block, panel), BF16),
        pltpu.VMEM((NX, NZ, 2, WINDOW, 128), F32),
        pltpu.VMEM((NZ, UNIT, 128), F32),
        pltpu.VMEM((NX, UNIT, 128), F32),
        pltpu.VMEM((KA, 2, NX, UNIT, 128), F32),
        pltpu.VMEM((KB, 2, NZ, UNIT, 128), F32),
        pltpu.VMEM((UNITS, 2, UNIT, 128), F32),
        pltpu.VMEM((PAIRS, 2, NY, 5, 8, 128), F32),
        pltpu.VMEM((PAIRS, NY, 5, 8, 128), F32),
        pltpu.VMEM((PAIRS, NY - 1, 5, 8, 128), F32),
        pltpu.VMEM((PAIRS, 4, 8, 128), F32),
        pltpu.VMEM((CHIPS, 8, 128), F32),
        pltpu.VMEM((PAIRS, 8, 128), F32),
        dma((CHIPS + 1,)), dma, dma((CHIPS + 1,)), dma, dma((2,)), dma,
        dma((PAIRS,)), dma((PAIRS,)), dma((PAIRS,)), dma((PAIRS,)), dma, dma,
    ]
    for shape in RINGS:
        scratch += Ring.scratch(*shape)
    scratch += Exchange.scratch(*EXCHANGES[0]) + HalfExchange.scratch(*EXCHANGES[1])
    gram, num = pl.pallas_call(
        functools.partial(kernel, scale),
        out_shape=(
            jax.ShapeDtypeStruct((WINDOW // NY, block), F32),
            jax.ShapeDtypeStruct((8, panel // 8), F32),
        ),
        in_specs=[pl.BlockSpec(memory_space=pl.ANY)] * 2,
        out_specs=(pl.BlockSpec(memory_space=pltpu.VMEM),) * 2,
        scratch_shapes=scratch,
        compiler_params=pltpu.CompilerParams(
            collective_id=0, has_side_effects=True, vmem_limit_bytes=60 * 2**20
        ),
    )(tokens, up_panel)
    return pl.pallas_call(
        write,
        out_shape=(
            jax.ShapeDtypeStruct((WINDOW // NY, block), F32),
            jax.ShapeDtypeStruct((1, panel), F32),
        ),
    )(gram, num)


def solution(mesh):
    return jax.shard_map(
        body,
        mesh=mesh,
        in_specs=(P("var", "tok", None), P("var", "tok", None)),
        out_specs=(P("var", "tok"), P(("var", "tok"), None)),
        check_vma=False,
    )
```
